32 devices in a mesh: expert: 16 (over z, y, x), dp: 2 (over core).
Axes of the slice: x: 2, y: 2, z: 4, core: 2. Of those that a mesh axis runs over, the one named last changes fastest.
Arguments:
- tokens: bfloat16 [4096, 2048], P(('dp', 'expert')), parts along dimension 0, may hold values from -6 to 6
- logits: float32 [4096, 16], P(('dp', 'expert')), parts along dimension 0, may hold values from -4 to 350
- weights: bfloat16 [16, 2048, 1024], P('expert'), may hold values from -0.125 to 0.125
- router_weight: bfloat16 [2048, 16], replicated, may hold values from -0.125 to 0.125
- expert_picks: int32 [32, 256], P(('dp', 'expert')), parts along dimension 0, may hold values from 0 to 2047, as said below
- cotangent: bfloat16 [32, 256, 1024], P(('dp', 'expert')), parts along dimension 0, may hold values from -1.5 to 1.5
Outputs:
- token_grad: bfloat16 [4096, 2048], P(('dp', 'expert')), parts along dimension 0
- weight_grad: bfloat16 [32, 2048, 1024], P(('dp', 'expert')), parts along dimension 0
- router_grad: float32 [4096, 16], P(('dp', 'expert')), parts along dimension 0
The draws below stay inside these ranges and needn't reach their ends.
There are 2 independent parts, one for each index of `dp`. The reference program is written for one: setup_inputs(seed, part) draws one part's arguments, and reference() takes and returns one part's arrays. A program takes and returns all parts, laid end to end along the dimension named above; an argument that names none is the same for every part. Nothing has to cross between parts.
Inputs may be any that keep to these rules, and one draw needn't show every extreme that they name: `expert_picks`: each expert's list is ascending and names no token twice. Among the tokens of one device (indices k * 128 to (k + 1) * 128 - 1) an expert takes at most 32, and in every draw each expert takes exactly 32 from some devices' tokens.
All inputs are finite; a program needn't handle non-finite values.
Results may differ from the reference program's by a relative error of at most 0.0062.
Values may be sent and summed in bfloat16 or wider, within the bound.
A program may use at most 64 MiB of HBM per device.

```python
import jax
import jax.numpy as jnp
from jax import lax

D = 2048
H = 1024
TOK_DEV = 128
EXPERTS = 16
TOKENS = 2048
CAP = 256
MOST = 32


def shuffle_owners(key_one):
    return jax.random.permutation(key_one, EXPERTS)


def shuffle_tokens(key_one):
    return jax.random.permutation(key_one, TOK_DEV)


def scatter_list(target_pos, token_vals):
    return jnp.zeros((CAP,), jnp.int32).at[target_pos.reshape(-1)].set(token_vals.reshape(-1), mode='drop')


def choose_picks(key):
    key_hot, key_score, key_tie, key_rows = jax.random.split(key, 4)
    per_owner = CAP // EXPERTS
    owner_heat = jax.random.randint(key_hot, (1, EXPERTS), 0, 4)
    jitter = jax.random.randint(key_score, (EXPERTS, EXPERTS), 0, 8)
    tie_break = jax.vmap(shuffle_owners)(jax.random.split(key_tie, EXPERTS)).astype(jnp.int32)
    score = (owner_heat * 8 + jitter) * EXPERTS + tie_break
    ranked = jnp.argsort(-score, axis=1)
    rank_of = jnp.argsort(ranked, axis=1)
    counts = jnp.where(rank_of < EXPERTS // 4, 2 * per_owner, jnp.where(rank_of < 3 * EXPERTS // 4, per_owner, 0))
    starts = jnp.cumsum(counts, axis=1) - counts
    shuffled = jax.vmap(shuffle_tokens)(jax.random.split(key_rows, EXPERTS * EXPERTS)).astype(jnp.int32)
    chosen = jnp.sort(shuffled[:, :MOST], axis=1).reshape(EXPERTS, EXPERTS, MOST)
    columns = jnp.arange(MOST, dtype=jnp.int32)[None, None, :]
    owners = jnp.arange(EXPERTS, dtype=jnp.int32)[None, :, None]
    target = jnp.where(columns < counts[:, :, None], starts[:, :, None] + columns, CAP)
    token_ids = owners * TOK_DEV + chosen
    return jax.vmap(scatter_list)(target, token_ids).astype(jnp.int32)


def draw_expert_picks(key, part):
    return choose_picks(key)


def draw_logits(key, part):
    picks_now = choose_picks(key)
    key = jax.random.fold_in(key, 5)
    key_base = jax.random.fold_in(key, 0)
    picked = jnp.zeros((TOKENS, EXPERTS), jnp.float32).at[picks_now, jnp.arange(EXPERTS)[:, None]].set(1.0)
    base_logits = jnp.clip(jax.random.normal(key_base, (TOKENS, EXPERTS), jnp.float32), -4.0, 4.0)
    scores = base_logits + 5.0 * picked
    return scores.astype(jnp.float32)


def spiked(drawn, stream_key, source, target, parts, factor):
    def block_of(dim):
        return (jnp.arange(drawn.shape[dim]) // (drawn.shape[dim] // parts)).reshape((-1,) + (1,) * (drawn.ndim - 1 - dim))

    one_side = jax.random.permutation(stream_key, parts)[block_of(target)]
    other_side = (block_of(target) + parts // 2) % parts
    return jnp.where((block_of(source) == one_side) | (block_of(source) == other_side), factor * drawn, drawn)


def steps_of(stream_key, shape, shards, least, top_value):
    level = 1.0
    for position, blocks in shards:
        heights = jax.random.uniform(jax.random.fold_in(jax.random.fold_in(stream_key, 6), position), (blocks,), jnp.float32, least / len(shards), top_value / len(shards))
        level = level * jnp.repeat(jnp.exp(heights), shape[position] // blocks).reshape((-1,) + (1,) * (len(shape) - 1 - position))
    return level


def noise(own_key, dims, scale, most, shards=(), kind=jnp.bfloat16):
    drawn = scale * jax.random.normal(own_key, dims, jnp.float32)
    if shards:
        drawn = drawn * steps_of(own_key, dims, shards, -0.22, 0.18)
    return jnp.clip(drawn, -most, most).astype(kind)


def gaussian_with(key, shape, deviation, bound, pieces, heavy, kind=jnp.bfloat16):
    entries = deviation * jax.random.normal(key, shape, jnp.float32)
    if pieces:
        entries = entries * steps_of(key, shape, pieces, -0.22, 0.18)
    return jnp.clip(spiked(entries, jax.random.fold_in(key, 3), *heavy), -bound, bound).astype(kind)


def setup_inputs(seed: int = 0, part: int = 0) -> dict:
    keys = jax.random.split(jax.random.key(seed), 7)
    part_keys = jax.random.split(jax.random.fold_in(keys[6], part), 7)
    return {
        "tokens": gaussian_with(part_keys[0], (TOKENS, D), 1.0, 6.0, ((0, 16),), (0, 1, 16, 2.0)),
        "logits": draw_logits(jax.random.fold_in(jax.random.fold_in(keys[6], part), 71), part),
        "weights": noise(keys[2], (EXPERTS, D, H), D ** -0.5, 0.125, ((0, 16),)),
        "router_weight": noise(keys[3], (D, EXPERTS), D ** -0.5, 0.125),
        "expert_picks": draw_expert_picks(jax.random.fold_in(jax.random.fold_in(keys[6], part), 71), part),
        "cotangent": noise(part_keys[5], (EXPERTS, CAP, H), 0.25, 1.5, ((0, 16),)),
    }


def reference(tokens, logits, weights, router_weight, expert_picks, cotangent):
    gate_probs = jax.nn.softmax(logits, axis=-1)
    gate_table = lax.optimization_barrier(gate_probs.astype(jnp.bfloat16))
    width = tokens.shape[1]

    def one_expert(running, inputs):
        expert_part, score_grad = running
        weight, wanted, upstream, expert_id = inputs
        picked_rows = jnp.take(tokens, wanted, axis=0)
        gate_vals = gate_table[wanted, expert_id].astype(jnp.float32)
        active = jnp.dot(picked_rows, weight, preferred_element_type=jnp.float32)
        gate_grad = jnp.sum(upstream.astype(jnp.float32) * active, axis=1).astype(jnp.bfloat16)
        gate_grad = lax.optimization_barrier(gate_grad).astype(jnp.float32)
        scaled = (gate_vals[:, None] * upstream.astype(jnp.float32)).astype(jnp.bfloat16)
        weight_grad = lax.dot_general(picked_rows, scaled, (((0,), (0,)), ((), ())), preferred_element_type=jnp.float32).astype(jnp.bfloat16)
        row_grad = lax.dot_general(scaled, weight, (((1,), (1,)), ((), ())), preferred_element_type=jnp.float32).astype(jnp.bfloat16)
        row_grad = lax.optimization_barrier(row_grad).astype(jnp.float32)
        expert_part = expert_part.at[wanted].add(row_grad)
        score_grad = score_grad.at[wanted, expert_id].add(gate_grad)
        return (expert_part, score_grad), weight_grad

    start = (jnp.zeros((TOKENS, width), jnp.float32), jnp.zeros((TOKENS, EXPERTS), jnp.float32))
    (expert_part, score_grad), weight_grad = lax.scan(one_expert, start, (weights, expert_picks, cotangent, jnp.arange(EXPERTS, dtype=jnp.int32)))
    inner_sum = jnp.sum(gate_probs * score_grad, axis=1, keepdims=True)
    logit_grad = (gate_probs * (score_grad - inner_sum)).astype(jnp.bfloat16)
    router_part = lax.dot_general(logit_grad, router_weight, (((1,), (1,)), ((), ())), preferred_element_type=jnp.float32)
    token_grad = (expert_part + router_part).astype(jnp.bfloat16)
    router_grad = lax.dot_general(tokens, logit_grad, (((0,), (0,)), ((), ())), preferred_element_type=jnp.float32)
    return (token_grad, weight_grad, router_grad)
```

```python
import functools
import math

import jax
import jax.numpy as jnp
from jax import lax
from jax.experimental import pallas as pl
from jax.experimental.pallas import tpu as pltpu
from jax.sharding import PartitionSpec as P

F32 = jnp.float32
BF16 = jnp.bfloat16
MESH = pl.DeviceIdType.MESH


def remote(src, dst, send, recv, peer):
    return pltpu.make_async_remote_copy(
        src_ref=src, dst_ref=dst, send_sem=send, recv_sem=recv,
        device_id={"expert": peer}, device_id_type=MESH)


def loop(low, high, body):
    def step(i, carry):
        body(i)
        return carry
    lax.fori_loop(low, high, step, 0)


def kernel(n, nz, most,
           tokens, logits_t, weights, router_t, cols, picks_row, placed_row, cot,
           token_grad, weight_grad, router_grad,
           wbuf, wgbuf, probs, info_src, info_dst, sel, sel_t, scaled, rg,
           tokbuf, fwd_src, rowbuf, bwd_src, bwdbuf, zin, zsend,
           score_src, score_dst, rs_src, rs_dst,
           w_sem, wg_sem, i_send, i_recv, a_send, a_recv, f_send, f_recv,
           b_send, b_recv, z_send, z_recv, s_send, s_recv, r_send, r_recv):
    plane = n // nz
    tok, width = tokens.shape
    hidden = cot.shape[1]
    cap = cot.shape[0]
    me = lax.axis_index("expert")
    z = me // plane
    c = me % plane

    w_copy = pltpu.make_async_copy(weights.at[0], wbuf, w_sem)
    w_copy.start()
    barrier = pltpu.get_barrier_semaphore()
    loop(1, n, lambda i: pl.semaphore_signal(
        barrier, inc=1, device_id={"expert": lax.rem(me + i, n)}, device_id_type=MESH))

    scores = logits_t[...]
    exps = jnp.exp(scores - jnp.max(scores, axis=0, keepdims=True))
    probs[...] = exps / jnp.sum(exps, axis=0, keepdims=True)
    info_src[...] = jnp.zeros_like(info_src)

    def fill_info(e):
        info_src[e, 0:1, :] = probs[pl.ds(e, 1), :]
        for k in range(cap // 128):
            info_src[e, 1 + k:2 + k, :] = picks_row[:, k * 128:(k + 1) * 128]
    loop(0, n, fill_info)
    info_dst[me] = info_src[me]
    pl.semaphore_wait(barrier, n - 1)

    def info_copy(peer):
        return remote(info_src.at[peer], info_dst.at[me], i_send.at[peer], i_recv.at[me], peer)

    def info_arrival(peer):
        return remote(info_src.at[peer], info_dst.at[peer], i_send.at[peer], i_recv.at[peer], peer)

    loop(1, n, lambda i: info_copy(lax.rem(me + i, n)).start())

    def up_own():
        return remote(tokens, tokbuf.at[z], a_send.at[0, z], a_recv.at[z], me + plane)

    def down_own():
        return remote(tokens, tokbuf.at[z], a_send.at[1, z], a_recv.at[z], me - plane)

    def up_pass(src):
        return remote(tokbuf.at[src], tokbuf.at[src], a_send.at[0, src], a_recv.at[src], me + plane)

    def down_pass(src):
        return remote(tokbuf.at[src], tokbuf.at[src], a_send.at[1, src], a_recv.at[src], me - plane)

    @pl.when(z < nz - 1)
    def _():
        up_own().start()

    @pl.when(z > 0)
    def _():
        down_own().start()

    loop(1, n, lambda i: info_arrival(lax.rem(me + i, n)).wait_recv())

    tok_col = lax.broadcasted_iota(jnp.int32, (tok, 128), 0).astype(F32)
    slot_lane = lax.broadcasted_iota(jnp.int32, (tok, plane * most), 1).astype(F32)

    def build_sel(zs):
        base = ((zs * plane + c) * tok).astype(F32)

        def one(e, acc):
            rank = jnp.zeros((tok, 128), F32)
            member = jnp.zeros((tok, 128), F32)
            for k in range(cap // 128):
                rel = info_dst[z * plane + e, 1 + k:2 + k, :] - base
                rank += jnp.where((rel >= 0.0) & (rel < tok_col), 1.0, 0.0)
                member += jnp.where(rel == tok_col, 1.0, 0.0)
            rank = jnp.sum(rank, axis=1, keepdims=True)
            member = jnp.sum(member, axis=1, keepdims=True)
            first = (e * most).astype(F32)
            return acc + jnp.where(slot_lane == rank + first, member, 0.0)

        made = lax.fori_loop(0, plane, one, jnp.zeros((tok, plane * most), F32))
        sel_t[zs] = made.astype(BF16)
        sel[zs] = made.T.astype(BF16)
    loop(0, nz, build_sel)

    def fwd_copy(zs, c2):
        return remote(fwd_src.at[zs, pl.ds(pl.multiple_of(c2 * most, most), most), :],
                      rowbuf.at[pl.ds(pl.multiple_of((zs * plane + c) * most, most), most), :],
                      f_send.at[zs, c2], f_recv.at[zs, c], z * plane + c2)

    def fwd_arrival(zs, c2):
        return remote(fwd_src.at[zs, pl.ds(pl.multiple_of(c2 * most, most), most), :],
                      rowbuf.at[pl.ds(pl.multiple_of((zs * plane + c2) * most, most), most), :],
                      f_send.at[zs, c2], f_recv.at[zs, c2], z * plane + c2)

    def forward(zs, block):
        tile = 512

        def piece(t):
            lanes = pl.ds(pl.multiple_of(t * tile, tile), tile)
            fwd_src[zs, :, lanes] = jnp.dot(
                sel[zs], block[:, lanes], preferred_element_type=F32).astype(BF16)
        loop(0, width // tile, piece)
        loop(1, plane, lambda i: fwd_copy(zs, lax.rem(c + i, plane)).start())
        rowbuf[pl.ds(pl.multiple_of((zs * plane + c) * most, most), most), :] = (
            fwd_src[zs, pl.ds(pl.multiple_of(c * most, most), most), :])

    forward(z, tokens)

    picks_col = cols[:, 0:1]
    placed_col = cols[:, 1:2]
    lane = lax.broadcasted_iota(jnp.int32, (cap, 128), 1).astype(F32)

    def add_gate(o, acc):
        hit = (picks_col - (o * tok).astype(F32)) == lane
        return acc + jnp.where(hit, info_dst[o, 0:1, :], 0.0)
    gate = jnp.sum(lax.fori_loop(0, n, add_gate, jnp.zeros((cap, 128), F32)), axis=1, keepdims=True)
    gate = gate.astype(BF16).astype(F32)
    scaled[...] = (gate * cot[...].astype(F32)).astype(BF16)
    w_copy.wait()

    def row_tile(t):
        lanes = pl.ds(pl.multiple_of(t * 256, 256), 256)
        rg[:, lanes] = lax.dot_general(
            scaled[...], wbuf[lanes, :], (((1,), (1,)), ((), ())),
            preferred_element_type=F32).astype(BF16)
    loop(0, width // 256, row_tile)

    def bwd_copy(zd, c2):
        return remote(bwd_src.at[zd, pl.ds(pl.multiple_of(c2 * most, most), most), :],
                      bwdbuf.at[zd, pl.ds(pl.multiple_of(c * most, most), most), :],
                      b_send.at[zd, c2], b_recv.at[zd, c], z * plane + c2)

    def bwd_arrival(zd, c2):
        return remote(bwd_src.at[zd, pl.ds(pl.multiple_of(c2 * most, most), most), :],
                      bwdbuf.at[zd, pl.ds(pl.multiple_of(c2 * most, most), most), :],
                      b_send.at[zd, c2], b_recv.at[zd, c2], z * plane + c2)

    slot_row = lax.broadcasted_iota(jnp.int32, (plane * most, cap), 0).astype(F32)

    def backward(zd):
        low = (zd * plane * most).astype(F32)
        spread = jnp.where(slot_row == placed_row[...] - low, 1.0, 0.0).astype(BF16)

        def piece(t):
            lanes = pl.ds(pl.multiple_of(t * 512, 512), 512)
            bwd_src[zd, :, lanes] = jnp.dot(
                spread, rg[:, lanes], preferred_element_type=F32).astype(BF16)
        loop(0, width // 512, piece)
        loop(1, plane, lambda i: bwd_copy(zd, lax.rem(c + i, plane)).start())
        mine = pl.ds(pl.multiple_of(c * most, most), most)
        bwdbuf[zd, mine, :] = bwd_src[zd, mine, :]

    for far in range(nz - 1, 0, -1):
        @pl.when(z + far < nz)
        def _(far=far):
            backward(z + far)

        @pl.when(z - far >= 0)
        def _(far=far):
            backward(z - far)
    backward(z)

    def chain(dest, slot, has_in, out_slot, peer):
        copy = remote(zsend.at[dest], zin.at[out_slot], z_send.at[dest], z_recv.at[out_slot], peer)
        loop(1, plane, lambda i: bwd_arrival(dest, lax.rem(c + i, plane)).wait_recv())

        @pl.when(has_in)
        def _():
            remote(zsend.at[dest], zin.at[slot], z_send.at[dest], z_recv.at[slot], peer).wait_recv()

            def piece(t):
                lanes = pl.ds(pl.multiple_of(t * 512, 512), 512)
                zsend[dest, :, lanes] = (jnp.dot(
                    sel_t[dest], bwdbuf[dest, :, lanes], preferred_element_type=F32)
                    + zin[slot, :, lanes].astype(F32)).astype(BF16)
            loop(0, width // 512, piece)

        @pl.when(jnp.logical_not(has_in))
        def _():
            def piece(t):
                lanes = pl.ds(pl.multiple_of(t * 512, 512), 512)
                zsend[dest, :, lanes] = jnp.dot(
                    sel_t[dest], bwdbuf[dest, :, lanes], preferred_element_type=F32).astype(BF16)
            loop(0, width // 512, piece)
        copy.start()

    for step in range(nz):
        if step > 0:
            @pl.when(z - step >= 0)
            def _(step=step):
                src = z - step
                up_pass(src).wait_recv()

                @pl.when(z < nz - 1)
                def _():
                    up_pass(src).start()
                forward(src, tokbuf.at[src])

            @pl.when(z + step < nz)
            def _(step=step):
                src = z + step
                down_pass(src).wait_recv()

                @pl.when(z > 0)
                def _():
                    down_pass(src).start()
                forward(src, tokbuf.at[src])

        up_dest = nz - 1 - (step - z)

        @pl.when((step >= z) & (up_dest > z))
        def _(up_dest=up_dest):
            chain(up_dest, up_dest, z > 0, up_dest, me + plane)

        down_dest = step - (nz - 1 - z)

        @pl.when((down_dest >= 0) & (down_dest < z))
        def _(down_dest=down_dest):
            chain(down_dest, down_dest, z < nz - 1,
                  jnp.where(down_dest == z - 1, nz, down_dest), me - plane)

    def rows_arrived(k):
        zs = k // plane
        c2 = k % plane

        @pl.when(c2 != c)
        def _():
            fwd_arrival(zs, c2).wait_recv()
    loop(0, n, rows_arrived)
    slot_lanes = lax.broadcasted_iota(jnp.int32, (cap, n * most), 1).astype(F32)
    compact = jnp.where(slot_lanes == placed_col, 1.0, 0.0).astype(BF16)

    rc = rg

    def compact_tile(t):
        lanes = pl.ds(pl.multiple_of(t * 256, 256), 256)
        rc[:, lanes] = jnp.dot(compact, rowbuf[:, lanes], preferred_element_type=F32).astype(BF16)
    loop(0, width // 256, compact_tile)

    def active_tile(t, acc):
        lanes = pl.ds(pl.multiple_of(t * 256, 256), 256)
        active = jnp.dot(rc[...], wbuf[:, lanes], preferred_element_type=F32)
        return acc + jnp.sum(cot[:, lanes].astype(F32) * active, axis=1, keepdims=True)
    gate_grad = lax.fori_loop(0, hidden // 256, active_tile, jnp.zeros((cap, 1), F32))
    gate_grad = gate_grad.astype(BF16).astype(F32)

    def score_copy(peer):
        return remote(score_src.at[peer], score_dst.at[me], s_send.at[peer], s_recv.at[me], peer)

    def score_arrival(peer):
        return remote(score_src.at[peer], score_dst.at[peer], s_send.at[peer], s_recv.at[peer], peer)

    score_src[...] = jnp.zeros_like(score_src)

    def score_row(i):
        o = lax.rem(me + i, n)
        hit = (picks_col - (o * tok).astype(F32)) == lane
        score_src[o, 0:1, :] = jnp.sum(jnp.where(hit, gate_grad, 0.0), axis=0, keepdims=True)

    def score_send(i):
        score_row(i)
        score_copy(lax.rem(me + i, n)).start()
    loop(1, n, score_send)
    score_row(0)
    score_dst[me] = score_src[me]

    def weight_tile(t):
        lanes = pl.ds(pl.multiple_of(t * 256, 256), 256)
        wgbuf[lanes, :] = lax.dot_general(
            rc[:, lanes], scaled[...], (((0,), (0,)), ((), ())),
            preferred_element_type=F32).astype(BF16)
    loop(0, width // 256, weight_tile)
    wg_copy = pltpu.make_async_copy(wgbuf, weight_grad.at[0], wg_sem)
    wg_copy.start()

    loop(1, n, lambda i: score_arrival(lax.rem(me + i, n)).wait_recv())
    score = score_dst[:, 0, :]
    prob = probs[...]
    inner = jnp.sum(prob * score, axis=0, keepdims=True)
    logit_grad = prob * (score - inner)
    logit_col = logit_grad.T.astype(BF16)
    logit_grad = logit_grad.astype(BF16)
    share = width // n
    wide = share % 128 == 0

    def router_tile(t):
        lanes = pl.ds(pl.multiple_of(t * 512, 512), 512)
        part = jnp.dot(logit_grad, tokens[:, lanes], preferred_element_type=F32)
        if wide:
            rs_src[:, lanes] = part
        else:
            rs_src[lanes, :] = part.T
    loop(0, width // 512, router_tile)

    def share_of(d):
        if wide:
            return rs_src.at[:, pl.ds(pl.multiple_of(d * share, share), share)]
        return rs_src.at[pl.ds(pl.multiple_of(d * share, share), share), :]

    def rs_copy(peer):
        return remote(share_of(peer), rs_dst.at[me], r_send.at[peer], r_recv.at[me], peer)

    def rs_arrival(peer):
        return remote(share_of(peer), rs_dst.at[peer], r_send.at[peer], r_recv.at[peer], peer)
    loop(1, n, lambda i: rs_copy(lax.rem(me + i, n)).start())
    rs_dst[me] = share_of(me)[...]

    loop(1, plane, lambda i: bwd_arrival(z, lax.rem(c + i, plane)).wait_recv())

    @pl.when(z == 0)
    def _():
        zin[z] = jnp.zeros(zin.shape[1:], BF16)

    @pl.when(z == nz - 1)
    def _():
        zin[nz] = jnp.zeros(zin.shape[1:], BF16)

    @pl.when(z > 0)
    def _():
        remote(zsend.at[z], zin.at[z], z_send.at[z], z_recv.at[z], me).wait_recv()

    @pl.when(z < nz - 1)
    def _():
        remote(zsend.at[z], zin.at[nz], z_send.at[z], z_recv.at[nz], me).wait_recv()

    def final_tile(t):
        lanes = pl.ds(pl.multiple_of(t * 512, 512), 512)
        total = jnp.dot(sel_t[z], bwdbuf[z, :, lanes], preferred_element_type=F32)
        total += zin[z, :, lanes].astype(F32) + zin[nz, :, lanes].astype(F32)
        total += jnp.dot(logit_col, router_t[:, lanes], preferred_element_type=F32)
        token_grad[:, lanes] = total.astype(BF16)
    loop(0, width // 512, final_tile)

    loop(1, n, lambda i: rs_arrival(lax.rem(me + i, n)).wait_recv())
    total = jnp.sum(rs_dst[...], axis=0)
    router_grad[...] = total.T if wide else total

    def sent(i):
        peer = lax.rem(me + i, n)
        info_copy(peer).wait_send()
        score_copy(peer).wait_send()
        rs_copy(peer).wait_send()
    loop(1, n, sent)

    def sent_plane(k):
        zs = k // plane
        c2 = k % plane

        @pl.when(c2 != c)
        def _():
            fwd_copy(zs, c2).wait_send()
            bwd_copy(zs, c2).wait_send()
    loop(0, n, sent_plane)

    def sent_z(zs):
        @pl.when((z < nz - 1) & (zs <= z))
        def _():
            up_pass(zs).wait_send()

        @pl.when((z > 0) & (zs >= z))
        def _():
            down_pass(zs).wait_send()

        @pl.when(zs != z)
        def _():
            remote(zsend.at[zs], zin.at[zs], z_send.at[zs], z_recv.at[zs], me).wait_send()
    loop(0, nz, sent_z)
    wg_copy.wait()


def local(tokens, logits, weights, router_weight, expert_picks, cotangent):
    n = lax.axis_size("expert")
    nz = 2 ** math.ceil(math.log2(n) / 3)
    plane = n // nz
    tok, width = tokens.shape
    cap = expert_picks.shape[1]
    hidden = weights.shape[2]
    slots = 2 * cap // n
    most = max(slots, 16)
    wanted = expert_picks[0]
    owner = wanted // tok
    before = jnp.sum((wanted[None, :] < (owner * tok)[:, None]).astype(jnp.int32), axis=1)
    placed = (owner * most + jnp.arange(cap, dtype=jnp.int32) - before).astype(F32)
    picks = wanted.astype(F32)
    cols = jnp.stack([picks, placed], axis=1)
    share = width // n
    rs_block = (n, share) if share % 128 == 0 else (share, n)
    rs_full = (n, width) if share % 128 == 0 else (width, n)
    vmem = pl.BlockSpec(memory_space=pltpu.VMEM)
    hbm = pl.BlockSpec(memory_space=pl.ANY)
    dma = pltpu.SemaphoreType.DMA
    flops = 2 * cap * width * hidden * 3
    return pl.pallas_call(
        functools.partial(kernel, n, nz, most),
        out_shape=(
            jax.ShapeDtypeStruct((tok, width), BF16),
            jax.ShapeDtypeStruct((1, width, hidden), BF16),
            jax.ShapeDtypeStruct((share, n), F32),
        ),
        in_specs=[vmem, vmem, hbm, vmem, vmem, vmem, vmem, vmem],
        out_specs=(vmem, hbm, vmem),
        scratch_shapes=[
            pltpu.VMEM((width, hidden), BF16),
            pltpu.VMEM((width, hidden), BF16),
            pltpu.VMEM((n, tok), F32),
            pltpu.VMEM((n, 8, 128), F32),
            pltpu.VMEM((n, 8, 128), F32),
            pltpu.VMEM((nz, plane * most, tok), BF16),
            pltpu.VMEM((nz, tok, plane * most), BF16),
            pltpu.VMEM((cap, hidden), BF16),
            pltpu.VMEM((cap, width), BF16),
            pltpu.VMEM((nz, tok, width), BF16),
            pltpu.VMEM((nz, plane * most, width), BF16),
            pltpu.VMEM((n * most, width), BF16),
            pltpu.VMEM((nz, plane * most, width), BF16),
            pltpu.VMEM((nz, plane * most, width), BF16),
            pltpu.VMEM((nz + 1, tok, width), BF16),
            pltpu.VMEM((nz, tok, width), BF16),
            pltpu.VMEM((n, 8, 128), F32),
            pltpu.VMEM((n, 8, 128), F32),
            pltpu.VMEM(rs_full, F32),
            pltpu.VMEM((n,) + rs_block, F32),
            dma, dma,
            dma((n,)), dma((n,)),
            dma((2, nz)), dma((nz,)),
            dma((nz, plane)), dma((nz, plane)),
            dma((nz, plane)), dma((nz, plane)),
            dma((nz,)), dma((nz + 1,)),
            dma((n,)), dma((n,)),
            dma((n,)), dma((n,)),
        ],
        compiler_params=pltpu.CompilerParams(
            collective_id=0, has_side_effects=True, vmem_limit_bytes=62 * 1024 * 1024),
        cost_estimate=pl.CostEstimate(flops=flops, bytes_accessed=12 * 2 ** 20, transcendentals=0),
    )(tokens, logits.T, weights, router_weight.T, cols, picks[None, :], placed[None, :], cotangent[0])


def solution(mesh):
    in_specs = (
        P(("dp", "expert"), None),
        P(("dp", "expert"), None),
        P("expert", None, None),
        P(),
        P(("dp", "expert"), None),
        P(("dp", "expert"), None, None),
    )
    out_specs = (
        P(("dp", "expert"), None),
        P(("dp", "expert"), None, None),
        P(("dp", "expert"), None),
    )
    return jax.shard_map(local, mesh=mesh, in_specs=in_specs, out_specs=out_specs, check_vma=False)
```

```python
import functools
import math

import jax
import jax.numpy as jnp
from jax import lax
from jax.experimental import pallas as pl
from jax.experimental.pallas import tpu as pltpu
from jax.sharding import PartitionSpec as P

F32 = jnp.float32
BF16 = jnp.bfloat16
MESH = pl.DeviceIdType.MESH
PARTS = 2


def remote(src, dst, send, recv, peer):
    return pltpu.make_async_remote_copy(
        src_ref=src, dst_ref=dst, send_sem=send, recv_sem=recv,
        device_id={"expert": peer}, device_id_type=MESH)


def loop(low, high, body):
    def step(i, carry):
        body(i)
        return carry
    lax.fori_loop(low, high, step, 0)


def kernel(n, nz, most, parts,
           tokens, logits_t, weights, router_t, picks_ref, cot,
           token_grad, rows_out, scaled_out, router_grad,
           wbuf, probs, info_src, info_dst, sel, sel_t, scaled, rg,
           tokbuf, fwd_src, rowbuf, bwd_src, bwdbuf, zin, zsend,
           score_src, score_dst, rs_src, rs_dst,
           w_sem, out_sem, i_send, i_recv, a_send, a_recv, f_send, f_recv,
           b_send, b_recv, z_send, z_recv, s_send, s_recv, r_send, r_recv):
    plane = n // nz
    tok, width = tokens.shape
    piece = width // parts
    tile = min(512, piece)
    hidden = cot.shape[1]
    cap = cot.shape[0]
    me = lax.axis_index("expert")
    z = me // plane
    c = me % plane
    group = plane * most

    w_copy = pltpu.make_async_copy(weights.at[0], wbuf, w_sem)
    w_copy.start()
    barrier = pltpu.get_barrier_semaphore()
    loop(1, n, lambda i: pl.semaphore_signal(
        barrier, inc=1, device_id={"expert": lax.rem(me + i, n)}, device_id_type=MESH))

    scores = logits_t[...]
    exps = jnp.exp(scores - jnp.max(scores, axis=0, keepdims=True))
    probs[...] = exps / jnp.sum(exps, axis=0, keepdims=True)
    picks_row = picks_ref[...].astype(F32)
    info_src[...] = jnp.zeros_like(info_src)

    def fill_info(e):
        info_src[e, 0:1, :] = probs[pl.ds(e, 1), :]
        for k in range(cap // 128):
            info_src[e, 1 + k:2 + k, :] = picks_row[:, k * 128:(k + 1) * 128]
    loop(0, n, fill_info)
    info_dst[me] = info_src[me]
    for h in range(parts):
        tokbuf[z, h] = tokens[:, h * piece:(h + 1) * piece]

    picks_wide = jnp.concatenate(
        [jnp.broadcast_to(picks_row[:, k * 128:(k + 1) * 128], (128, 128)).T
         for k in range(cap // 128)], axis=0)
    picks_col = picks_wide[:, 0:1]

    def padded(values, other, axis, order):
        owner = jnp.floor(values * (1.0 / tok))
        before = jnp.sum(jnp.where(other < owner * tok, 1.0, 0.0), axis=axis, keepdims=True)
        return owner * most + order.astype(F32) - before
    placed_col = padded(picks_col, picks_row, 1, lax.broadcasted_iota(jnp.int32, (cap, 1), 0))
    placed_row = padded(picks_row, picks_col, 0, lax.broadcasted_iota(jnp.int32, (1, cap), 1))
    pl.semaphore_wait(barrier, n - 1)

    def info_copy(peer):
        return remote(info_src.at[peer], info_dst.at[me], i_send.at[peer], i_recv.at[me], peer)

    def info_arrival(peer):
        return remote(info_src.at[peer], info_dst.at[peer], i_send.at[peer], i_recv.at[peer], peer)

    loop(1, n, lambda i: info_copy(lax.rem(me + i, n)).start())

    def next_of(way):
        return me + plane * (1 - 2 * way)

    def goes_on(way):
        return jnp.where(way == 0, z < nz - 1, z > 0)

    def token_copy(way, src, h):
        return remote(tokbuf.at[src, h], tokbuf.at[src, h],
                      a_send.at[way, src, h], a_recv.at[src, h], next_of(way))

    def token_start(k):
        way, h = k % 2, k // 2

        @pl.when(goes_on(way))
        def _():
            token_copy(way, z, h).start()
    loop(0, 2 * parts, token_start)
    loop(1, n, lambda i: info_arrival(lax.rem(me + i, n)).wait_recv())

    lane = lax.broadcasted_iota(jnp.int32, (cap, 128), 1).astype(F32)

    def add_gate(o, acc):
        hit = (picks_col - (o * tok).astype(F32)) == lane
        return acc + jnp.where(hit, info_dst[o, 0:1, :], 0.0)
    gate = jnp.sum(lax.fori_loop(0, n, add_gate, jnp.zeros((cap, 128), F32)), axis=1, keepdims=True)
    gate = gate.astype(BF16).astype(F32)
    scaled[...] = (gate * cot[...].astype(F32)).astype(BF16)
    scaled_copy = pltpu.make_async_copy(scaled, scaled_out, out_sem.at[0])
    scaled_copy.start()
    w_copy.wait()

    def row_tile(t):
        rows = pl.ds(pl.multiple_of(t * tile, tile), tile)
        per = piece // tile
        lanes = pl.ds(pl.multiple_of((t % per) * tile, tile), tile)
        rg[t // per, :, lanes] = lax.dot_general(
            scaled[...], wbuf[rows, :], (((1,), (1,)), ((), ())),
            preferred_element_type=F32).astype(BF16)
    loop(0, width // tile, row_tile)

    def mine_of(c2):
        return pl.ds(pl.multiple_of(c2 * most, most), most)

    def bwd_copy(zd, h, c2):
        return remote(bwd_src.at[zd, h, mine_of(c2), :], bwdbuf.at[zd, h, mine_of(c), :],
                      b_send.at[zd, h, c2], b_recv.at[zd, h, c], z * plane + c2)

    def bwd_arrival(zd, h, c2):
        return remote(bwd_src.at[zd, h, mine_of(c2), :], bwdbuf.at[zd, h, mine_of(c2), :],
                      b_send.at[zd, h, c2], b_recv.at[zd, h, c2], z * plane + c2)

    slot_row = lax.broadcasted_iota(jnp.int32, (group, cap), 0).astype(F32)

    def backward(zd, h):
        low = (zd * group).astype(F32)
        spread = jnp.where(slot_row == placed_row - low, 1.0, 0.0).astype(BF16)
        for t in range(piece // tile):
            lanes = slice(t * tile, (t + 1) * tile)
            bwd_src[zd, h, :, lanes] = jnp.dot(
                spread, rg[h, :, lanes], preferred_element_type=F32).astype(BF16)
        loop(1, plane, lambda i: bwd_copy(zd, h, lax.rem(c + i, plane)).start())
        bwdbuf[zd, h, mine_of(c), :] = bwd_src[zd, h, mine_of(c), :]

    def chain_place(q, way):
        start = jnp.where(way == 0, z, nz - 1 - z)
        k = q - start
        block = jnp.maximum(k, 0) // parts
        dest = jnp.where(way == 0, nz - 1 - block, block)
        valid = (k >= 0) & (block < nz - 1 - start)
        return valid, jnp.minimum(jnp.maximum(dest, 0), nz - 1), jnp.maximum(k, 0) % parts, start > 0

    def backward_at(q):
        def one(way):
            valid, dest, h, _ = chain_place(q, way)

            @pl.when(valid)
            def _():
                backward(dest, h)
        loop(0, 2, one)

    ahead = parts
    loop(0, ahead, backward_at)

    tok_col = lax.broadcasted_iota(jnp.int32, (tok, 128), 0).astype(F32)
    slot_lane = lax.broadcasted_iota(jnp.int32, (tok, group), 1).astype(F32)

    def build_sel(zs):
        base = ((zs * plane + c) * tok).astype(F32)

        def one(e, acc):
            rank = jnp.zeros((tok, 128), F32)
            member = jnp.zeros((tok, 128), F32)
            for k in range(cap // 128):
                rel = info_dst[z * plane + e, 1 + k:2 + k, :] - base
                rank += jnp.where((rel >= 0.0) & (rel < tok_col), 1.0, 0.0)
                member += jnp.where(rel == tok_col, 1.0, 0.0)
            rank = jnp.sum(rank, axis=1, keepdims=True)
            member = jnp.sum(member, axis=1, keepdims=True)
            first = (e * most).astype(F32)
            return acc + jnp.where(slot_lane == rank + first, member, 0.0)

        made = lax.fori_loop(0, plane, one, jnp.zeros((tok, group), F32))
        sel_t[zs] = made.astype(BF16)
        sel[zs] = made.T.astype(BF16)
    loop(0, nz, build_sel)

    def rows_of(zs, c2):
        return pl.ds(pl.multiple_of((zs * plane + c2) * most, most), most)

    def fwd_copy(zs, h, c2):
        return remote(fwd_src.at[zs, h, mine_of(c2), :], rowbuf.at[h, rows_of(zs, c), :],
                      f_send.at[zs, h, c2], f_recv.at[zs, h, c], z * plane + c2)

    def fwd_arrival(zs, h, c2):
        return remote(fwd_src.at[zs, h, mine_of(c2), :], rowbuf.at[h, rows_of(zs, c2), :],
                      f_send.at[zs, h, c2], f_recv.at[zs, h, c2], z * plane + c2)

    def forward_at(q, way):
        far, h = q // parts, q % parts
        src = z + (2 * way - 1) * far

        @pl.when((src >= 0) & (src < nz) & ((far > 0) | (way == 0)))
        def _():
            @pl.when(far > 0)
            def _():
                token_copy(way, src, h).wait_recv()

                @pl.when(goes_on(way))
                def _():
                    token_copy(way, src, h).start()
            for t in range(piece // tile):
                lanes = slice(t * tile, (t + 1) * tile)
                fwd_src[src, h, :, lanes] = jnp.dot(
                    sel[src], tokbuf[src, h, :, lanes], preferred_element_type=F32).astype(BF16)
            loop(1, plane, lambda i: fwd_copy(src, h, lax.rem(c + i, plane)).start())
            rowbuf[h, rows_of(src, c), :] = fwd_src[src, h, mine_of(c), :]

    def chain_at(q, way):
        valid, dest, h, has_in = chain_place(q, way)
        out_slot = jnp.where((way == 1) & (dest == z - 1), nz, dest)

        @pl.when(valid)
        def _():
            loop(1, plane, lambda i: bwd_arrival(dest, h, lax.rem(c + i, plane)).wait_recv())

            @pl.when(has_in)
            def _():
                remote(zsend.at[dest, h], zin.at[dest, h], z_send.at[dest, h],
                       z_recv.at[dest, h], me).wait_recv()

            @pl.when(jnp.logical_not(has_in))
            def _():
                zin[dest, h] = jnp.zeros(zin.shape[2:], BF16)
            for t in range(piece // tile):
                lanes = slice(t * tile, (t + 1) * tile)
                zsend[dest, h, :, lanes] = (jnp.dot(
                    sel_t[dest], bwdbuf[dest, h, :, lanes], preferred_element_type=F32)
                    + zin[dest, h, :, lanes].astype(F32)).astype(BF16)
            remote(zsend.at[dest, h], zin.at[out_slot, h], z_send.at[dest, h],
                   z_recv.at[out_slot, h], next_of(way)).start()

    def substep(q):
        loop(0, 2, lambda way: forward_at(q, way))
        backward_at(q + ahead)

        @pl.when((q >= parts * (nz - 2)) & (q < parts * (nz - 1)))
        def _():
            backward(z, q % parts)
        loop(0, 2, lambda way: chain_at(q, way))
    loop(0, nz * parts, substep)

    slot_lanes = lax.broadcasted_iota(jnp.int32, (cap, n * most), 1).astype(F32)
    compact = jnp.where(slot_lanes == placed_col, 1.0, 0.0).astype(BF16)
    rc = rg

    def gate_part(h, total):
        def rows_arrived(k):
            zs = k // plane
            c2 = k % plane

            @pl.when(c2 != c)
            def _():
                fwd_arrival(zs, h, c2).wait_recv()
        loop(0, n, rows_arrived)
        for t in range(piece // tile):
            lanes = slice(t * tile, (t + 1) * tile)
            rc[h, :, lanes] = jnp.dot(
                compact, rowbuf[h, :, lanes], preferred_element_type=F32).astype(BF16)

        def active_tile(t, acc):
            lanes = pl.ds(pl.multiple_of(t * 256, 256), 256)
            depth = pl.ds(pl.multiple_of(h * piece, piece), piece)
            active = jnp.dot(rc[h], wbuf[depth, lanes], preferred_element_type=F32)
            return acc + jnp.sum(cot[:, lanes].astype(F32) * active, axis=1, keepdims=True)
        return lax.fori_loop(0, hidden // 256, active_tile, total)
    gate_grad = lax.fori_loop(0, parts, gate_part, jnp.zeros((cap, 1), F32))
    gate_grad = gate_grad.astype(BF16).astype(F32)
    rows_copy = pltpu.make_async_copy(rc, rows_out, out_sem.at[1])
    rows_copy.start()

    def score_copy(peer):
        return remote(score_src.at[peer], score_dst.at[me], s_send.at[peer], s_recv.at[me], peer)

    def score_arrival(peer):
        return remote(score_src.at[peer], score_dst.at[peer], s_send.at[peer], s_recv.at[peer], peer)

    score_src[...] = jnp.zeros_like(score_src)

    def score_row(i):
        o = lax.rem(me + i, n)
        hit = (picks_col - (o * tok).astype(F32)) == lane
        score_src[o, 0:1, :] = jnp.sum(jnp.where(hit, gate_grad, 0.0), axis=0, keepdims=True)

    def score_send(i):
        score_row(i)
        score_copy(lax.rem(me + i, n)).start()
    loop(1, n, score_send)
    score_row(0)
    score_dst[me] = score_src[me]

    def own_back(h):
        loop(1, plane, lambda i: bwd_arrival(z, h, lax.rem(c + i, plane)).wait_recv())

        @pl.when(z == 0)
        def _():
            zin[z, h] = jnp.zeros(zin.shape[2:], BF16)

        @pl.when(z == nz - 1)
        def _():
            zin[nz, h] = jnp.zeros(zin.shape[2:], BF16)

        @pl.when(z > 0)
        def _():
            remote(zsend.at[z, h], zin.at[z, h], z_send.at[z, h], z_recv.at[z, h], me).wait_recv()

        @pl.when(z < nz - 1)
        def _():
            remote(zsend.at[z, h], zin.at[nz, h], z_send.at[z, h], z_recv.at[nz, h], me).wait_recv()
    loop(1, n, lambda i: score_arrival(lax.rem(me + i, n)).wait_recv())
    score = score_dst[:, 0, :]
    prob = probs[...]
    inner = jnp.sum(prob * score, axis=0, keepdims=True)
    logit_grad = prob * (score - inner)
    logit_col = logit_grad.T.astype(BF16)
    logit_grad = logit_grad.astype(BF16)
    share = width // n
    wide = share % 128 == 0

    def router_tile(t):
        lanes = pl.ds(pl.multiple_of(t * 512, 512), 512)
        part = jnp.dot(logit_grad, tokens[:, lanes], preferred_element_type=F32)
        if wide:
            rs_src[:, lanes] = part
        else:
            rs_src[lanes, :] = part.T
    loop(0, width // 512, router_tile)

    def share_of(d):
        if wide:
            return rs_src.at[:, pl.ds(pl.multiple_of(d * share, share), share)]
        return rs_src.at[pl.ds(pl.multiple_of(d * share, share), share), :]

    def rs_copy(peer):
        return remote(share_of(peer), rs_dst.at[me], r_send.at[peer], r_recv.at[me], peer)

    def rs_arrival(peer):
        return remote(share_of(peer), rs_dst.at[peer], r_send.at[peer], r_recv.at[peer], peer)
    loop(1, n, lambda i: rs_copy(lax.rem(me + i, n)).start())
    rs_dst[me] = share_of(me)[...]

    def final_part(h):
        own_back(h)
        for t in range(piece // tile):
            lanes = slice(t * tile, (t + 1) * tile)
            whole = pl.ds(pl.multiple_of(h * piece + t * tile, tile), tile)
            total = jnp.dot(sel_t[z], bwdbuf[z, h, :, lanes], preferred_element_type=F32)
            total += zin[z, h, :, lanes].astype(F32) + zin[nz, h, :, lanes].astype(F32)
            total += jnp.dot(logit_col, router_t[:, whole], preferred_element_type=F32)
            token_grad[:, whole] = total.astype(BF16)
    loop(0, parts, final_part)

    loop(1, n, lambda i: rs_arrival(lax.rem(me + i, n)).wait_recv())
    total = jnp.sum(rs_dst[...], axis=0)
    router_grad[...] = total.T if wide else total

    def sent(i):
        peer = lax.rem(me + i, n)
        info_copy(peer).wait_send()
        score_copy(peer).wait_send()
        rs_copy(peer).wait_send()
    loop(1, n, sent)

    def sent_plane(k):
        zs = k // (plane * parts)
        h = (k // plane) % parts
        c2 = k % plane

        @pl.when(c2 != c)
        def _():
            fwd_copy(zs, h, c2).wait_send()
            bwd_copy(zs, h, c2).wait_send()
    loop(0, n * parts, sent_plane)

    def sent_z(k):
        zs, h = k // parts, k % parts

        @pl.when((z < nz - 1) & (zs <= z))
        def _():
            token_copy(0, zs, h).wait_send()

        @pl.when((z > 0) & (zs >= z))
        def _():
            token_copy(1, zs, h).wait_send()

        @pl.when(zs != z)
        def _():
            remote(zsend.at[zs, h], zin.at[zs, h], z_send.at[zs, h], z_recv.at[zs, h], me).wait_send()
    loop(0, nz * parts, sent_z)
    scaled_copy.wait()
    rows_copy.wait()


def finish(rows, scaled, token_in, router_in, weight_grad, token_grad, router_grad):
    weight_grad[0] = lax.dot_general(
        rows[0], scaled[...], (((0,), (0,)), ((), ())), preferred_element_type=F32).astype(BF16)
    token_grad[...] = token_in[...]
    router_grad[...] = router_in[...]


def local(tokens, logits, weights, router_weight, expert_picks, cotangent):
    n = lax.axis_size("expert")
    nz = 2 ** math.ceil(math.log2(n) / 3)
    parts = PARTS
    plane = n // nz
    tok, width = tokens.shape
    piece = width // parts
    cap = expert_picks.shape[1]
    hidden = weights.shape[2]
    most = max(2 * cap // n, 16)
    share = width // n
    rs_block = (n, share) if share % 128 == 0 else (share, n)
    rs_full = (n, width) if share % 128 == 0 else (width, n)
    vmem = pl.BlockSpec(memory_space=pltpu.VMEM)
    hbm = pl.BlockSpec(memory_space=pl.ANY)
    dma = pltpu.SemaphoreType.DMA
    flops = 2 * cap * width * hidden * 2
    token_in, rows, scaled, router_in = pl.pallas_call(
        functools.partial(kernel, n, nz, most, parts),
        out_shape=(
            jax.ShapeDtypeStruct((tok, width), BF16),
            jax.ShapeDtypeStruct((parts, cap, piece), BF16),
            jax.ShapeDtypeStruct((cap, hidden), BF16),
            jax.ShapeDtypeStruct((share, n), F32),
        ),
        in_specs=[vmem, vmem, hbm, vmem, vmem, vmem],
        out_specs=(vmem, hbm, hbm, vmem),
        scratch_shapes=[
            pltpu.VMEM((width, hidden), BF16),
            pltpu.VMEM((n, tok), F32),
            pltpu.VMEM((n, 8, 128), F32),
            pltpu.VMEM((n, 8, 128), F32),
            pltpu.VMEM((nz, plane * most, tok), BF16),
            pltpu.VMEM((nz, tok, plane * most), BF16),
            pltpu.VMEM((cap, hidden), BF16),
            pltpu.VMEM((parts, cap, piece), BF16),
            pltpu.VMEM((nz, parts, tok, piece), BF16),
            pltpu.VMEM((nz, parts, plane * most, piece), BF16),
            pltpu.VMEM((parts, n * most, piece), BF16),
            pltpu.VMEM((nz, parts, plane * most, piece), BF16),
            pltpu.VMEM((nz, parts, plane * most, piece), BF16),
            pltpu.VMEM((nz + 1, parts, tok, piece), BF16),
            pltpu.VMEM((nz, parts, tok, piece), BF16),
            pltpu.VMEM((n, 8, 128), F32),
            pltpu.VMEM((n, 8, 128), F32),
            pltpu.VMEM(rs_full, F32),
            pltpu.VMEM((n,) + rs_block, F32),
            dma, dma((2,)),
            dma((n,)), dma((n,)),
            dma((2, nz, parts)), dma((nz, parts)),
            dma((nz, parts, plane)), dma((nz, parts, plane)),
            dma((nz, parts, plane)), dma((nz, parts, plane)),
            dma((nz, parts)), dma((nz + 1, parts)),
            dma((n,)), dma((n,)),
            dma((n,)), dma((n,)),
        ],
        compiler_params=pltpu.CompilerParams(
            collective_id=0, has_side_effects=True, vmem_limit_bytes=62 * 1024 * 1024),
        cost_estimate=pl.CostEstimate(flops=flops, bytes_accessed=8 * 2 ** 20, transcendentals=0),
    )(tokens, logits.T, weights, router_weight.T, expert_picks, cotangent[0])
    block = min(512, piece)
    per = piece // block
    weight_grad, token_grad, router_grad = pl.pallas_call(
        finish,
        grid=(width // block,),
        out_shape=(
            jax.ShapeDtypeStruct((1, width, hidden), BF16),
            jax.ShapeDtypeStruct((tok, width), BF16),
            jax.ShapeDtypeStruct((share, n), F32),
        ),
        in_specs=[
            pl.BlockSpec((1, cap, block), lambda i: (i // per, 0, i % per)),
            pl.BlockSpec((cap, hidden), lambda i: (0, 0)),
            pl.BlockSpec((tok, block), lambda i: (0, i)),
            pl.BlockSpec((share, n), lambda i: (0, 0)),
        ],
        out_specs=(
            pl.BlockSpec((1, block, hidden), lambda i: (0, i, 0)),
            pl.BlockSpec((tok, block), lambda i: (0, i)),
            pl.BlockSpec((share, n), lambda i: (0, 0)),
        ),
        compiler_params=pltpu.CompilerParams(vmem_limit_bytes=32 * 1024 * 1024),
        cost_estimate=pl.CostEstimate(
            flops=flops // 2, bytes_accessed=7 * 2 ** 20, transcendentals=0),
    )(rows, scaled, token_in, router_in)
    return token_grad, weight_grad, router_grad


def solution(mesh):
    in_specs = (
        P(("dp", "expert"), None),
        P(("dp", "expert"), None),
        P("expert", None, None),
        P(),
        P(("dp", "expert"), None),
        P(("dp", "expert"), None, None),
    )
    out_specs = (
        P(("dp", "expert"), None),
        P(("dp", "expert"), None, None),
        P(("dp", "expert"), None),
    )
    return jax.shard_map(local, mesh=mesh, in_specs=in_specs, out_specs=out_specs, check_vma=False)
```

```python
import functools
import math

import jax
import jax.numpy as jnp
from jax import lax
from jax.experimental import pallas as pl
from jax.experimental.pallas import tpu as pltpu
from jax.sharding import PartitionSpec as P

F32 = jnp.float32
BF16 = jnp.bfloat16
MESH = pl.DeviceIdType.MESH
PARTS = 2


def remote(src, dst, send, recv, peer):
    return pltpu.make_async_remote_copy(
        src_ref=src, dst_ref=dst, send_sem=send, recv_sem=recv,
        device_id={"expert": peer}, device_id_type=MESH)


def loop(low, high, body):
    def step(i, carry):
        body(i)
        return carry
    lax.fori_loop(low, high, step, 0)


def kernel(n, nz, most, parts,
           tokens, logits_t, weights, router_t, picks_ref, cot,
           token_grad, rows_out, scaled_out, router_grad,
           wbuf, probs, info_src, info_dst, sel, sel_t, scaled, rg,
           tokbuf, fwd_src, rowbuf, bwd_src, bwdbuf, zin, zsend,
           score_src, score_dst, rs_src, rs_dst,
           w_sem, out_sem, i_send, i_recv, a_send, a_recv, f_send, f_recv,
           b_send, b_recv, z_send, z_recv, s_send, s_recv, r_send, r_recv):
    plane = n // nz
    tok, width = tokens.shape
    piece = width // parts
    tile = min(512, piece)
    hidden = cot.shape[1]
    cap = cot.shape[0]
    me = lax.axis_index("expert")
    z = me // plane
    c = me % plane
    group = plane * most

    w_copy = pltpu.make_async_copy(weights.at[0], wbuf, w_sem)
    w_copy.start()
    barrier = pltpu.get_barrier_semaphore()
    loop(1, n, lambda i: pl.semaphore_signal(
        barrier, inc=1, device_id={"expert": lax.rem(me + i, n)}, device_id_type=MESH))

    scores = logits_t[...]
    exps = jnp.exp(scores - jnp.max(scores, axis=0, keepdims=True))
    probs[...] = exps / jnp.sum(exps, axis=0, keepdims=True)
    picks_row = picks_ref[...].astype(F32)
    info_src[...] = jnp.zeros_like(info_src)

    def fill_info(e):
        info_src[e, 0:1, :] = probs[pl.ds(e, 1), :]
        for k in range(cap // 128):
            info_src[e, 1 + k:2 + k, :] = picks_row[:, k * 128:(k + 1) * 128]
    loop(0, n, fill_info)
    info_dst[me] = info_src[me]
    for h in range(parts):
        tokbuf[z, h] = tokens[:, h * piece:(h + 1) * piece]

    picks_wide = jnp.concatenate(
        [jnp.broadcast_to(picks_row[:, k * 128:(k + 1) * 128], (128, 128)).T
         for k in range(cap // 128)], axis=0)
    picks_col = picks_wide[:, 0:1]

    def padded(values, other, axis, order):
        owner = jnp.floor(values * (1.0 / tok))
        before = jnp.sum(jnp.where(other < owner * tok, 1.0, 0.0), axis=axis, keepdims=True)
        return owner * most + order.astype(F32) - before
    placed_col = padded(picks_col, picks_row, 1, lax.broadcasted_iota(jnp.int32, (cap, 1), 0))
    placed_row = padded(picks_row, picks_col, 0, lax.broadcasted_iota(jnp.int32, (1, cap), 1))
    pl.semaphore_wait(barrier, n - 1)

    def info_copy(peer):
        return remote(info_src.at[peer], info_dst.at[me], i_send.at[peer], i_recv.at[me], peer)

    def info_arrival(peer):
        return remote(info_src.at[peer], info_dst.at[peer], i_send.at[peer], i_recv.at[peer], peer)

    loop(1, n, lambda i: info_copy(lax.rem(me + i, n)).start())

    def next_of(way):
        return me + plane * (1 - 2 * way)

    def goes_on(way):
        return jnp.where(way == 0, z < nz - 1, z > 0)

    def token_copy(way, src, h):
        return remote(tokbuf.at[src, h], tokbuf.at[src, h],
                      a_send.at[way, src, h], a_recv.at[src, h], next_of(way))

    def token_start(k):
        way, h = k % 2, k // 2

        @pl.when(goes_on(way))
        def _():
            token_copy(way, z, h).start()
    loop(0, 2 * parts, token_start)
    loop(1, n, lambda i: info_arrival(lax.rem(me + i, n)).wait_recv())

    lane = lax.broadcasted_iota(jnp.int32, (cap, 128), 1).astype(F32)

    def add_gate(o, acc):
        hit = (picks_col - (o * tok).astype(F32)) == lane
        return acc + jnp.where(hit, info_dst[o, 0:1, :], 0.0)
    gate = jnp.sum(lax.fori_loop(0, n, add_gate, jnp.zeros((cap, 128), F32)), axis=1, keepdims=True)
    gate = gate.astype(BF16).astype(F32)
    scaled[...] = (gate * cot[...].astype(F32)).astype(BF16)
    scaled_copy = pltpu.make_async_copy(scaled, scaled_out, out_sem.at[0])
    scaled_copy.start()
    w_copy.wait()

    def row_tile(t):
        rows = pl.ds(pl.multiple_of(t * tile, tile), tile)
        per = piece // tile
        lanes = pl.ds(pl.multiple_of((t % per) * tile, tile), tile)
        rg[t // per, :, lanes] = lax.dot_general(
            scaled[...], wbuf[rows, :], (((1,), (1,)), ((), ())),
            preferred_element_type=F32).astype(BF16)
    loop(0, width // tile, row_tile)

    def mine_of(c2):
        return pl.ds(pl.multiple_of(c2 * most, most), most)

    def bwd_copy(zd, h, c2):
        return remote(bwd_src.at[zd, h, mine_of(c2), :], bwdbuf.at[zd, h, mine_of(c), :],
                      b_send.at[zd, h, c2], b_recv.at[zd, h, c], z * plane + c2)

    def bwd_arrival(zd, h, c2):
        return remote(bwd_src.at[zd, h, mine_of(c2), :], bwdbuf.at[zd, h, mine_of(c2), :],
                      b_send.at[zd, h, c2], b_recv.at[zd, h, c2], z * plane + c2)

    slot_row = lax.broadcasted_iota(jnp.int32, (group, cap), 0).astype(F32)

    def backward(zd, h):
        low = (zd * group).astype(F32)
        spread = jnp.where(slot_row == placed_row - low, 1.0, 0.0).astype(BF16)
        for t in range(piece // tile):
            lanes = slice(t * tile, (t + 1) * tile)
            bwd_src[zd, h, :, lanes] = jnp.dot(
                spread, rg[h, :, lanes], preferred_element_type=F32).astype(BF16)
        loop(1, plane, lambda i: bwd_copy(zd, h, lax.rem(c + i, plane)).start())
        bwdbuf[zd, h, mine_of(c), :] = bwd_src[zd, h, mine_of(c), :]

    def chain_place(q, way):
        start = jnp.where(way == 0, z, nz - 1 - z)
        k = q - start
        block = jnp.maximum(k, 0) // parts
        dest = jnp.where(way == 0, nz - 1 - block, block)
        valid = (k >= 0) & (block < nz - 1 - start)
        return valid, jnp.minimum(jnp.maximum(dest, 0), nz - 1), jnp.maximum(k, 0) % parts, start > 0

    def backward_at(q):
        def one(way):
            valid, dest, h, _ = chain_place(q, way)

            @pl.when(valid)
            def _():
                backward(dest, h)
        loop(0, 2, one)

    late = parts + 1
    loop(0, parts, backward_at)

    tok_col = lax.broadcasted_iota(jnp.int32, (tok, 128), 0).astype(F32)
    slot_lane = lax.broadcasted_iota(jnp.int32, (tok, group), 1).astype(F32)

    def build_sel(zs):
        base = ((zs * plane + c) * tok).astype(F32)

        def one(e, acc):
            rank = jnp.zeros((tok, 128), F32)
            member = jnp.zeros((tok, 128), F32)
            for k in range(cap // 128):
                rel = info_dst[z * plane + e, 1 + k:2 + k, :] - base
                rank += jnp.where((rel >= 0.0) & (rel < tok_col), 1.0, 0.0)
                member += jnp.where(rel == tok_col, 1.0, 0.0)
            rank = jnp.sum(rank, axis=1, keepdims=True)
            member = jnp.sum(member, axis=1, keepdims=True)
            first = (e * most).astype(F32)
            return acc + jnp.where(slot_lane == rank + first, member, 0.0)

        made = lax.fori_loop(0, plane, one, jnp.zeros((tok, group), F32))
        sel_t[zs] = made.astype(BF16)
        sel[zs] = made.T.astype(BF16)
    loop(0, nz, build_sel)

    def rows_of(zs, c2):
        return pl.ds(pl.multiple_of((zs * plane + c2) * most, most), most)

    def fwd_copy(zs, h, c2):
        return remote(fwd_src.at[zs, h, mine_of(c2), :], rowbuf.at[h, rows_of(zs, c), :],
                      f_send.at[zs, h, c2], f_recv.at[zs, h, c], z * plane + c2)

    def fwd_arrival(zs, h, c2):
        return remote(fwd_src.at[zs, h, mine_of(c2), :], rowbuf.at[h, rows_of(zs, c2), :],
                      f_send.at[zs, h, c2], f_recv.at[zs, h, c2], z * plane + c2)

    def forward_at(q, way):
        far, h = q // parts, q % parts
        src = z + (2 * way - 1) * far

        @pl.when((src >= 0) & (src < nz) & ((far > 0) | (way == 0)))
        def _():
            @pl.when(far > 0)
            def _():
                token_copy(way, src, h).wait_recv()

                @pl.when(goes_on(way))
                def _():
                    token_copy(way, src, h).start()
            for t in range(piece // tile):
                lanes = slice(t * tile, (t + 1) * tile)
                fwd_src[src, h, :, lanes] = jnp.dot(
                    sel[src], tokbuf[src, h, :, lanes], preferred_element_type=F32).astype(BF16)
            loop(1, plane, lambda i: fwd_copy(src, h, lax.rem(c + i, plane)).start())
            rowbuf[h, rows_of(src, c), :] = fwd_src[src, h, mine_of(c), :]

    def chain_at(q, way):
        valid, dest, h, has_in = chain_place(q, way)
        out_slot = jnp.where((way == 1) & (dest == z - 1), nz, dest)

        @pl.when(valid)
        def _():
            loop(1, plane, lambda i: bwd_arrival(dest, h, lax.rem(c + i, plane)).wait_recv())

            @pl.when(has_in)
            def _():
                remote(zsend.at[dest, h], zin.at[dest, h], z_send.at[dest, h],
                       z_recv.at[dest, h], me).wait_recv()

            @pl.when(jnp.logical_not(has_in))
            def _():
                zin[dest, h] = jnp.zeros(zin.shape[2:], BF16)
            for t in range(piece // tile):
                lanes = slice(t * tile, (t + 1) * tile)
                zsend[dest, h, :, lanes] = (jnp.dot(
                    sel_t[dest], bwdbuf[dest, h, :, lanes], preferred_element_type=F32)
                    + zin[dest, h, :, lanes].astype(F32)).astype(BF16)
            remote(zsend.at[dest, h], zin.at[out_slot, h], z_send.at[dest, h],
                   z_recv.at[out_slot, h], next_of(way)).start()

    def substep(q):
        loop(0, 2, lambda way: forward_at(q, way))
        backward_at(q + parts)

        @pl.when((q >= parts * (nz - 2)) & (q < parts * (nz - 1)))
        def _():
            backward(z, q % parts)
        loop(0, 2, lambda way: chain_at(q - late, way))
    loop(0, nz * parts + late, substep)

    slot_lanes = lax.broadcasted_iota(jnp.int32, (cap, n * most), 1).astype(F32)
    compact = jnp.where(slot_lanes == placed_col, 1.0, 0.0).astype(BF16)
    rc = rg

    def gate_part(h, total):
        def rows_arrived(k):
            zs = k // plane
            c2 = k % plane

            @pl.when(c2 != c)
            def _():
                fwd_arrival(zs, h, c2).wait_recv()
        loop(0, n, rows_arrived)
        for t in range(piece // tile):
            lanes = slice(t * tile, (t + 1) * tile)
            rc[h, :, lanes] = jnp.dot(
                compact, rowbuf[h, :, lanes], preferred_element_type=F32).astype(BF16)

        def active_tile(t, acc):
            lanes = pl.ds(pl.multiple_of(t * 256, 256), 256)
            depth = pl.ds(pl.multiple_of(h * piece, piece), piece)
            active = jnp.dot(rc[h], wbuf[depth, lanes], preferred_element_type=F32)
            return acc + jnp.sum(cot[:, lanes].astype(F32) * active, axis=1, keepdims=True)
        return lax.fori_loop(0, hidden // 256, active_tile, total)
    gate_grad = lax.fori_loop(0, parts, gate_part, jnp.zeros((cap, 1), F32))
    gate_grad = gate_grad.astype(BF16).astype(F32)
    rows_copy = pltpu.make_async_copy(rc, rows_out, out_sem.at[1])
    rows_copy.start()

    def score_copy(peer):
        return remote(score_src.at[peer], score_dst.at[me], s_send.at[peer], s_recv.at[me], peer)

    def score_arrival(peer):
        return remote(score_src.at[peer], score_dst.at[peer], s_send.at[peer], s_recv.at[peer], peer)

    score_src[...] = jnp.zeros_like(score_src)

    def score_row(i):
        o = lax.rem(me + i, n)
        hit = (picks_col - (o * tok).astype(F32)) == lane
        score_src[o, 0:1, :] = jnp.sum(jnp.where(hit, gate_grad, 0.0), axis=0, keepdims=True)

    def score_send(i):
        score_row(i)
        score_copy(lax.rem(me + i, n)).start()
    loop(1, n, score_send)
    score_row(0)
    score_dst[me] = score_src[me]

    def own_back(h):
        loop(1, plane, lambda i: bwd_arrival(z, h, lax.rem(c + i, plane)).wait_recv())

        @pl.when(z == 0)
        def _():
            zin[z, h] = jnp.zeros(zin.shape[2:], BF16)

        @pl.when(z == nz - 1)
        def _():
            zin[nz, h] = jnp.zeros(zin.shape[2:], BF16)

        @pl.when(z > 0)
        def _():
            remote(zsend.at[z, h], zin.at[z, h], z_send.at[z, h], z_recv.at[z, h], me).wait_recv()

        @pl.when(z < nz - 1)
        def _():
            remote(zsend.at[z, h], zin.at[nz, h], z_send.at[z, h], z_recv.at[nz, h], me).wait_recv()
    loop(1, n, lambda i: score_arrival(lax.rem(me + i, n)).wait_recv())
    score = score_dst[:, 0, :]
    prob = probs[...]
    inner = jnp.sum(prob * score, axis=0, keepdims=True)
    logit_grad = prob * (score - inner)
    logit_col = logit_grad.T.astype(BF16)
    logit_grad = logit_grad.astype(BF16)
    share = width // n
    wide = share % 128 == 0

    def router_tile(t):
        lanes = pl.ds(pl.multiple_of(t * 512, 512), 512)
        part = jnp.dot(logit_grad, tokens[:, lanes], preferred_element_type=F32)
        if wide:
            rs_src[:, lanes] = part
        else:
            rs_src[lanes, :] = part.T
    loop(0, width // 512, router_tile)

    def share_of(d):
        if wide:
            return rs_src.at[:, pl.ds(pl.multiple_of(d * share, share), share)]
        return rs_src.at[pl.ds(pl.multiple_of(d * share, share), share), :]

    def rs_copy(peer):
        return remote(share_of(peer), rs_dst.at[me], r_send.at[peer], r_recv.at[me], peer)

    def rs_arrival(peer):
        return remote(share_of(peer), rs_dst.at[peer], r_send.at[peer], r_recv.at[peer], peer)
    loop(1, n, lambda i: rs_copy(lax.rem(me + i, n)).start())
    rs_dst[me] = share_of(me)[...]

    def final_part(h):
        own_back(h)
        for t in range(piece // tile):
            lanes = slice(t * tile, (t + 1) * tile)
            whole = pl.ds(pl.multiple_of(h * piece + t * tile, tile), tile)
            total = jnp.dot(sel_t[z], bwdbuf[z, h, :, lanes], preferred_element_type=F32)
            total += zin[z, h, :, lanes].astype(F32) + zin[nz, h, :, lanes].astype(F32)
            total += jnp.dot(logit_col, router_t[:, whole], preferred_element_type=F32)
            token_grad[:, whole] = total.astype(BF16)
    loop(0, parts, final_part)

    loop(1, n, lambda i: rs_arrival(lax.rem(me + i, n)).wait_recv())
    total = jnp.sum(rs_dst[...], axis=0)
    router_grad[...] = total

    def sent(i):
        peer = lax.rem(me + i, n)
        info_copy(peer).wait_send()
        score_copy(peer).wait_send()
        rs_copy(peer).wait_send()
    loop(1, n, sent)

    def sent_plane(k):
        zs = k // (plane * parts)
        h = (k // plane) % parts
        c2 = k % plane

        @pl.when(c2 != c)
        def _():
            fwd_copy(zs, h, c2).wait_send()
            bwd_copy(zs, h, c2).wait_send()
    loop(0, n * parts, sent_plane)

    def sent_z(k):
        zs, h = k // parts, k % parts

        @pl.when((z < nz - 1) & (zs <= z))
        def _():
            token_copy(0, zs, h).wait_send()

        @pl.when((z > 0) & (zs >= z))
        def _():
            token_copy(1, zs, h).wait_send()

        @pl.when(zs != z)
        def _():
            remote(zsend.at[zs, h], zin.at[zs, h], z_send.at[zs, h], z_recv.at[zs, h], me).wait_send()
    loop(0, nz * parts, sent_z)
    scaled_copy.wait()
    rows_copy.wait()


def finish(rows, scaled, token_in, router_in, weight_grad, token_grad, router_grad):
    weight_grad[0] = lax.dot_general(
        rows[0], scaled[...], (((0,), (0,)), ((), ())), preferred_element_type=F32).astype(BF16)
    token_grad[...] = token_in[...]
    router_grad[...] = router_in[...]


def local(tokens, logits, weights, router_weight, expert_picks, cotangent):
    n = lax.axis_size("expert")
    nz = 2 ** math.ceil(math.log2(n) / 3)
    parts = PARTS
    plane = n // nz
    tok, width = tokens.shape
    piece = width // parts
    cap = expert_picks.shape[1]
    hidden = weights.shape[2]
    most = max(2 * cap // n, 16)
    share = width // n
    rs_block = (n, share) if share % 128 == 0 else (share, n)
    rs_full = (n, width) if share % 128 == 0 else (width, n)
    vmem = pl.BlockSpec(memory_space=pltpu.VMEM)
    hbm = pl.BlockSpec(memory_space=pl.ANY)
    dma = pltpu.SemaphoreType.DMA
    flops = 2 * cap * width * hidden * 2
    token_in, rows, scaled, router_in = pl.pallas_call(
        functools.partial(kernel, n, nz, most, parts),
        out_shape=(
            jax.ShapeDtypeStruct((tok, width), BF16),
            jax.ShapeDtypeStruct((parts, cap, piece), BF16),
            jax.ShapeDtypeStruct((cap, hidden), BF16),
            jax.ShapeDtypeStruct(rs_block, F32),
        ),
        in_specs=[vmem, vmem, hbm, vmem, vmem, vmem],
        out_specs=(vmem, hbm, hbm, vmem),
        scratch_shapes=[
            pltpu.VMEM((width, hidden), BF16),
            pltpu.VMEM((n, tok), F32),
            pltpu.VMEM((n, 8, 128), F32),
            pltpu.VMEM((n, 8, 128), F32),
            pltpu.VMEM((nz, plane * most, tok), BF16),
            pltpu.VMEM((nz, tok, plane * most), BF16),
            pltpu.VMEM((cap, hidden), BF16),
            pltpu.VMEM((parts, cap, piece), BF16),
            pltpu.VMEM((nz, parts, tok, piece), BF16),
            pltpu.VMEM((nz, parts, plane * most, piece), BF16),
            pltpu.VMEM((parts, n * most, piece), BF16),
            pltpu.VMEM((nz, parts, plane * most, piece), BF16),
            pltpu.VMEM((nz, parts, plane * most, piece), BF16),
            pltpu.VMEM((nz + 1, parts, tok, piece), BF16),
            pltpu.VMEM((nz, parts, tok, piece), BF16),
            pltpu.VMEM((n, 8, 128), F32),
            pltpu.VMEM((n, 8, 128), F32),
            pltpu.VMEM(rs_full, F32),
            pltpu.VMEM((n,) + rs_block, F32),
            dma, dma((2,)),
            dma((n,)), dma((n,)),
            dma((2, nz, parts)), dma((nz, parts)),
            dma((nz, parts, plane)), dma((nz, parts, plane)),
            dma((nz, parts, plane)), dma((nz, parts, plane)),
            dma((nz, parts)), dma((nz + 1, parts)),
            dma((n,)), dma((n,)),
            dma((n,)), dma((n,)),
        ],
        compiler_params=pltpu.CompilerParams(
            collective_id=0, has_side_effects=True, vmem_limit_bytes=62 * 1024 * 1024),
        cost_estimate=pl.CostEstimate(flops=flops, bytes_accessed=8 * 2 ** 20, transcendentals=0),
    )(tokens, logits.T, weights, router_weight.T, expert_picks, cotangent[0])
    block = min(512, piece)
    per = piece // block
    weight_grad, token_grad, router_grad = pl.pallas_call(
        finish,
        grid=(width // block,),
        out_shape=(
            jax.ShapeDtypeStruct((1, width, hidden), BF16),
            jax.ShapeDtypeStruct((tok, width), BF16),
            jax.ShapeDtypeStruct(rs_block, F32),
        ),
        in_specs=[
            pl.BlockSpec((1, cap, block), lambda i: (i // per, 0, i % per)),
            pl.BlockSpec((cap, hidden), lambda i: (0, 0)),
            pl.BlockSpec((tok, block), lambda i: (0, i)),
            pl.BlockSpec(rs_block, lambda i: (0, 0)),
        ],
        out_specs=(
            pl.BlockSpec((1, block, hidden), lambda i: (0, i, 0)),
            pl.BlockSpec((tok, block), lambda i: (0, i)),
            pl.BlockSpec(rs_block, lambda i: (0, 0)),
        ),
        compiler_params=pltpu.CompilerParams(vmem_limit_bytes=62 * 1024 * 1024),
        cost_estimate=pl.CostEstimate(
            flops=flops // 2, bytes_accessed=7 * 2 ** 20, transcendentals=0),
    )(rows, scaled, token_in, router_in)
    return token_grad, weight_grad, router_grad.T if share % 128 == 0 else router_grad


def solution(mesh):
    in_specs = (
        P(("dp", "expert"), None),
        P(("dp", "expert"), None),
        P("expert", None, None),
        P(),
        P(("dp", "expert"), None),
        P(("dp", "expert"), None, None),
    )
    out_specs = (
        P(("dp", "expert"), None),
        P(("dp", "expert"), None, None),
        P(("dp", "expert"), None),
    )
    return jax.shard_map(local, mesh=mesh, in_specs=in_specs, out_specs=out_specs, check_vma=False)
```

```python
import functools
import math

import jax
import jax.numpy as jnp
from jax import lax
from jax.experimental import pallas as pl
from jax.experimental.pallas import tpu as pltpu
from jax.sharding import PartitionSpec as P

F32 = jnp.float32
BF16 = jnp.bfloat16
MESH = pl.DeviceIdType.MESH
PARTS = 2


def remote(src, dst, send, recv, peer):
    return pltpu.make_async_remote_copy(
        src_ref=src, dst_ref=dst, send_sem=send, recv_sem=recv,
        device_id={"expert": peer}, device_id_type=MESH)


def loop(low, high, body):
    def step(i, carry):
        body(i)
        return carry
    lax.fori_loop(low, high, step, 0)


def kernel(n, nz, most, parts,
           tokens, logits_t, weights, router_t, picks_ref, cot,
           token_grad, rows_out, scaled_out, router_grad,
           wbuf, probs, info_src, info_dst, sel, sel_t, scaled, rg,
           tokbuf, fwd_src, rowbuf, bwd_src, bwdbuf, zin, zsend,
           score_src, score_dst, rs_src, rs_dst,
           w_sem, out_sem, i_send, i_recv, a_send, a_recv, f_send, f_recv,
           b_send, b_recv, z_send, z_recv, s_send, s_recv, r_send, r_recv):
    plane = n // nz
    tok, width = tokens.shape
    piece = width // parts
    tile = min(512, piece)
    hidden = cot.shape[1]
    cap = cot.shape[0]
    me = lax.axis_index("expert")
    z = me // plane
    c = me % plane
    group = plane * most

    w_copy = pltpu.make_async_copy(weights.at[0], wbuf, w_sem)
    w_copy.start()
    barrier = pltpu.get_barrier_semaphore()
    loop(1, n, lambda i: pl.semaphore_signal(
        barrier, inc=1, device_id={"expert": lax.rem(me + i, n)}, device_id_type=MESH))

    scores = logits_t[...]
    exps = jnp.exp(scores - jnp.max(scores, axis=0, keepdims=True))
    probs[...] = exps / jnp.sum(exps, axis=0, keepdims=True)
    picks_row = picks_ref[...].astype(F32)
    info_src[...] = jnp.zeros_like(info_src)

    def fill_info(e):
        info_src[e, 0:1, :] = probs[pl.ds(e, 1), :]
        for k in range(cap // 128):
            info_src[e, 1 + k:2 + k, :] = picks_row[:, k * 128:(k + 1) * 128]
    loop(0, n, fill_info)
    info_dst[me] = info_src[me]
    for h in range(parts):
        tokbuf[z, h] = tokens[:, h * piece:(h + 1) * piece]

    picks_wide = jnp.concatenate(
        [jnp.broadcast_to(picks_row[:, k * 128:(k + 1) * 128], (128, 128)).T
         for k in range(cap // 128)], axis=0)
    picks_col = picks_wide[:, 0:1]

    def padded(values, other, axis, order):
        owner = jnp.floor(values * (1.0 / tok))
        before = jnp.sum(jnp.where(other < owner * tok, 1.0, 0.0), axis=axis, keepdims=True)
        return owner * most + order.astype(F32) - before
    placed_col = padded(picks_col, picks_row, 1, lax.broadcasted_iota(jnp.int32, (cap, 1), 0))
    placed_row = padded(picks_row, picks_col, 0, lax.broadcasted_iota(jnp.int32, (1, cap), 1))
    pl.semaphore_wait(barrier, n - 1)

    def info_copy(peer):
        return remote(info_src.at[peer], info_dst.at[me], i_send.at[peer], i_recv.at[me], peer)

    def info_arrival(peer):
        return remote(info_src.at[peer], info_dst.at[peer], i_send.at[peer], i_recv.at[peer], peer)

    loop(1, n, lambda i: info_copy(lax.rem(me + i, n)).start())

    def next_of(way):
        return me + plane * (1 - 2 * way)

    def goes_on(way):
        return jnp.where(way == 0, z < nz - 1, z > 0)

    def token_copy(way, src, h):
        return remote(tokbuf.at[src, h], tokbuf.at[src, h],
                      a_send.at[way, src, h], a_recv.at[src, h], next_of(way))

    def token_start(k):
        way, h = k % 2, k // 2

        @pl.when(goes_on(way))
        def _():
            token_copy(way, z, h).start()
    loop(0, 2 * parts, token_start)
    loop(1, n, lambda i: info_arrival(lax.rem(me + i, n)).wait_recv())

    def mine_of(c2):
        return pl.ds(pl.multiple_of(c2 * most, most), most)

    tok_col = lax.broadcasted_iota(jnp.int32, (tok, 128), 0).astype(F32)
    slot_lane = lax.broadcasted_iota(jnp.int32, (tok, group), 1).astype(F32)

    def build_sel(zs):
        base = ((zs * plane + c) * tok).astype(F32)

        def one(e, acc):
            rank = jnp.zeros((tok, 128), F32)
            member = jnp.zeros((tok, 128), F32)
            for k in range(cap // 128):
                rel = info_dst[z * plane + e, 1 + k:2 + k, :] - base
                rank += jnp.where((rel >= 0.0) & (rel < tok_col), 1.0, 0.0)
                member += jnp.where(rel == tok_col, 1.0, 0.0)
            rank = jnp.sum(rank, axis=1, keepdims=True)
            member = jnp.sum(member, axis=1, keepdims=True)
            first = (e * most).astype(F32)
            return acc + jnp.where(slot_lane == rank + first, member, 0.0)

        made = lax.fori_loop(0, plane, one, jnp.zeros((tok, group), F32))
        sel_t[zs] = made.astype(BF16)
        sel[zs] = made.T.astype(BF16)

    def rows_of(zs, c2):
        return pl.ds(pl.multiple_of((zs * plane + c2) * most, most), most)

    def fwd_copy(zs, h, c2):
        return remote(fwd_src.at[zs, h, mine_of(c2), :], rowbuf.at[h, rows_of(zs, c), :],
                      f_send.at[zs, h, c2], f_recv.at[zs, h, c], z * plane + c2)

    def fwd_arrival(zs, h, c2):
        return remote(fwd_src.at[zs, h, mine_of(c2), :], rowbuf.at[h, rows_of(zs, c2), :],
                      f_send.at[zs, h, c2], f_recv.at[zs, h, c2], z * plane + c2)

    def pick_rows(src, h):
        for t in range(piece // tile):
            lanes = slice(t * tile, (t + 1) * tile)
            fwd_src[src, h, :, lanes] = jnp.dot(
                sel[src], tokbuf[src, h, :, lanes], preferred_element_type=F32).astype(BF16)
        loop(1, plane, lambda i: fwd_copy(src, h, lax.rem(c + i, plane)).start())
        rowbuf[h, rows_of(src, c), :] = fwd_src[src, h, mine_of(c), :]

    build_sel(z)
    loop(0, parts, lambda h: pick_rows(z, h))

    lane = lax.broadcasted_iota(jnp.int32, (cap, 128), 1).astype(F32)

    def add_gate(o, acc):
        hit = (picks_col - (o * tok).astype(F32)) == lane
        return acc + jnp.where(hit, info_dst[o, 0:1, :], 0.0)
    gate = jnp.sum(lax.fori_loop(0, n, add_gate, jnp.zeros((cap, 128), F32)), axis=1, keepdims=True)
    gate = gate.astype(BF16).astype(F32)
    scaled[...] = (gate * cot[...].astype(F32)).astype(BF16)
    scaled_copy = pltpu.make_async_copy(scaled, scaled_out, out_sem.at[0])
    scaled_copy.start()
    w_copy.wait()

    def row_tile(t):
        rows = pl.ds(pl.multiple_of(t * tile, tile), tile)
        per = piece // tile
        lanes = pl.ds(pl.multiple_of((t % per) * tile, tile), tile)
        rg[t // per, :, lanes] = lax.dot_general(
            scaled[...], wbuf[rows, :], (((1,), (1,)), ((), ())),
            preferred_element_type=F32).astype(BF16)
    loop(0, width // tile, row_tile)

    def bwd_copy(zd, h, c2):
        return remote(bwd_src.at[zd, h, mine_of(c2), :], bwdbuf.at[zd, h, mine_of(c), :],
                      b_send.at[zd, h, c2], b_recv.at[zd, h, c], z * plane + c2)

    def bwd_arrival(zd, h, c2):
        return remote(bwd_src.at[zd, h, mine_of(c2), :], bwdbuf.at[zd, h, mine_of(c2), :],
                      b_send.at[zd, h, c2], b_recv.at[zd, h, c2], z * plane + c2)

    slot_row = lax.broadcasted_iota(jnp.int32, (group, cap), 0).astype(F32)

    def backward(zd, h):
        low = (zd * group).astype(F32)
        spread = jnp.where(slot_row == placed_row - low, 1.0, 0.0).astype(BF16)
        for t in range(piece // tile):
            lanes = slice(t * tile, (t + 1) * tile)
            bwd_src[zd, h, :, lanes] = jnp.dot(
                spread, rg[h, :, lanes], preferred_element_type=F32).astype(BF16)
        loop(1, plane, lambda i: bwd_copy(zd, h, lax.rem(c + i, plane)).start())
        bwdbuf[zd, h, mine_of(c), :] = bwd_src[zd, h, mine_of(c), :]

    def chain_place(q, way):
        start = jnp.where(way == 0, z, nz - 1 - z)
        k = q - start
        block = jnp.maximum(k, 0) // parts
        dest = jnp.where(way == 0, nz - 1 - block, block)
        valid = (k >= 0) & (block < nz - 1 - start)
        return valid, jnp.minimum(jnp.maximum(dest, 0), nz - 1), jnp.maximum(k, 0) % parts, start > 0

    def backward_at(q):
        def one(way):
            valid, dest, h, _ = chain_place(q, way)

            @pl.when(valid)
            def _():
                backward(dest, h)
        loop(0, 2, one)

    late = parts + 1
    loop(0, parts, backward_at)

    loop(1, nz, lambda k: build_sel(lax.rem(z + k, nz)))

    def forward_at(q, way):
        far, h = q // parts, q % parts
        src = z + (2 * way - 1) * far

        @pl.when((src >= 0) & (src < nz) & (far > 0))
        def _():
            token_copy(way, src, h).wait_recv()

            @pl.when(goes_on(way))
            def _():
                token_copy(way, src, h).start()
            pick_rows(src, h)

    def chain_at(q, way):
        valid, dest, h, has_in = chain_place(q, way)
        out_slot = jnp.where((way == 1) & (dest == z - 1), nz, dest)

        @pl.when(valid)
        def _():
            loop(1, plane, lambda i: bwd_arrival(dest, h, lax.rem(c + i, plane)).wait_recv())

            @pl.when(has_in)
            def _():
                remote(zsend.at[dest, h], zin.at[dest, h], z_send.at[dest, h],
                       z_recv.at[dest, h], me).wait_recv()

            @pl.when(jnp.logical_not(has_in))
            def _():
                zin[dest, h] = jnp.zeros(zin.shape[2:], BF16)
            for t in range(piece // tile):
                lanes = slice(t * tile, (t + 1) * tile)
                zsend[dest, h, :, lanes] = (jnp.dot(
                    sel_t[dest], bwdbuf[dest, h, :, lanes], preferred_element_type=F32)
                    + zin[dest, h, :, lanes].astype(F32)).astype(BF16)
            remote(zsend.at[dest, h], zin.at[out_slot, h], z_send.at[dest, h],
                   z_recv.at[out_slot, h], next_of(way)).start()

    def substep(q):
        loop(0, 2, lambda way: forward_at(q, way))
        backward_at(q + parts)

        @pl.when((q >= parts * nz - 1) & (q < parts * nz + parts - 1))
        def _():
            backward(z, q - (parts * nz - 1))
        loop(0, 2, lambda way: chain_at(q - late, way))
    loop(0, nz * parts + late, substep)

    slot_lanes = lax.broadcasted_iota(jnp.int32, (cap, n * most), 1).astype(F32)
    compact = jnp.where(slot_lanes == placed_col, 1.0, 0.0).astype(BF16)
    rc = rg

    def gate_part(h, total):
        def rows_arrived(k):
            zs = k // plane
            c2 = k % plane

            @pl.when(c2 != c)
            def _():
                fwd_arrival(zs, h, c2).wait_recv()
        loop(0, n, rows_arrived)
        for t in range(piece // tile):
            lanes = slice(t * tile, (t + 1) * tile)
            rc[h, :, lanes] = jnp.dot(
                compact, rowbuf[h, :, lanes], preferred_element_type=F32).astype(BF16)

        def active_tile(t, acc):
            lanes = pl.ds(pl.multiple_of(t * 256, 256), 256)
            depth = pl.ds(pl.multiple_of(h * piece, piece), piece)
            active = jnp.dot(rc[h], wbuf[depth, lanes], preferred_element_type=F32)
            return acc + jnp.sum(cot[:, lanes].astype(F32) * active, axis=1, keepdims=True)
        return lax.fori_loop(0, hidden // 256, active_tile, total)
    gate_grad = lax.fori_loop(0, parts, gate_part, jnp.zeros((cap, 1), F32))
    gate_grad = gate_grad.astype(BF16).astype(F32)
    rows_copy = pltpu.make_async_copy(rc, rows_out, out_sem.at[1])
    rows_copy.start()

    def score_copy(peer):
        return remote(score_src.at[peer], score_dst.at[me], s_send.at[peer], s_recv.at[me], peer)

    def score_arrival(peer):
        return remote(score_src.at[peer], score_dst.at[peer], s_send.at[peer], s_recv.at[peer], peer)

    score_src[...] = jnp.zeros_like(score_src)

    def score_row(i):
        o = lax.rem(me + i, n)
        hit = (picks_col - (o * tok).astype(F32)) == lane
        score_src[o, 0:1, :] = jnp.sum(jnp.where(hit, gate_grad, 0.0), axis=0, keepdims=True)

    def score_send(i):
        score_row(i)
        score_copy(lax.rem(me + i, n)).start()
    loop(1, n, score_send)
    score_row(0)
    score_dst[me] = score_src[me]

    def own_back(h):
        loop(1, plane, lambda i: bwd_arrival(z, h, lax.rem(c + i, plane)).wait_recv())

        @pl.when(z == 0)
        def _():
            zin[z, h] = jnp.zeros(zin.shape[2:], BF16)

        @pl.when(z == nz - 1)
        def _():
            zin[nz, h] = jnp.zeros(zin.shape[2:], BF16)

        @pl.when(z > 0)
        def _():
            remote(zsend.at[z, h], zin.at[z, h], z_send.at[z, h], z_recv.at[z, h], me).wait_recv()

        @pl.when(z < nz - 1)
        def _():
            remote(zsend.at[z, h], zin.at[nz, h], z_send.at[z, h], z_recv.at[nz, h], me).wait_recv()
    loop(1, n, lambda i: score_arrival(lax.rem(me + i, n)).wait_recv())
    score = score_dst[:, 0, :]
    prob = probs[...]
    inner = jnp.sum(prob * score, axis=0, keepdims=True)
    logit_grad = prob * (score - inner)
    logit_col = logit_grad.T.astype(BF16)
    logit_grad = logit_grad.astype(BF16)
    share = width // n
    wide = share % 128 == 0

    def router_tile(t):
        lanes = pl.ds(pl.multiple_of(t * 512, 512), 512)
        part = jnp.dot(logit_grad, tokens[:, lanes], preferred_element_type=F32)
        if wide:
            rs_src[:, lanes] = part
        else:
            rs_src[lanes, :] = part.T
    loop(0, width // 512, router_tile)

    def share_of(d):
        if wide:
            return rs_src.at[:, pl.ds(pl.multiple_of(d * share, share), share)]
        return rs_src.at[pl.ds(pl.multiple_of(d * share, share), share), :]

    def rs_copy(peer):
        return remote(share_of(peer), rs_dst.at[me], r_send.at[peer], r_recv.at[me], peer)

    def rs_arrival(peer):
        return remote(share_of(peer), rs_dst.at[peer], r_send.at[peer], r_recv.at[peer], peer)
    loop(1, n, lambda i: rs_copy(lax.rem(me + i, n)).start())
    rs_dst[me] = share_of(me)[...]

    def final_part(h):
        own_back(h)
        for t in range(piece // tile):
            lanes = slice(t * tile, (t + 1) * tile)
            whole = pl.ds(pl.multiple_of(h * piece + t * tile, tile), tile)
            total = jnp.dot(sel_t[z], bwdbuf[z, h, :, lanes], preferred_element_type=F32)
            total += zin[z, h, :, lanes].astype(F32) + zin[nz, h, :, lanes].astype(F32)
            total += jnp.dot(logit_col, router_t[:, whole], preferred_element_type=F32)
            token_grad[:, whole] = total.astype(BF16)
    loop(0, parts, final_part)

    loop(1, n, lambda i: rs_arrival(lax.rem(me + i, n)).wait_recv())
    total = jnp.sum(rs_dst[...], axis=0)
    router_grad[...] = total

    def sent(i):
        peer = lax.rem(me + i, n)
        info_copy(peer).wait_send()
        score_copy(peer).wait_send()
        rs_copy(peer).wait_send()
    loop(1, n, sent)

    def sent_plane(k):
        zs = k // (plane * parts)
        h = (k // plane) % parts
        c2 = k % plane

        @pl.when(c2 != c)
        def _():
            fwd_copy(zs, h, c2).wait_send()
            bwd_copy(zs, h, c2).wait_send()
    loop(0, n * parts, sent_plane)

    def sent_z(k):
        zs, h = k // parts, k % parts

        @pl.when((z < nz - 1) & (zs <= z))
        def _():
            token_copy(0, zs, h).wait_send()

        @pl.when((z > 0) & (zs >= z))
        def _():
            token_copy(1, zs, h).wait_send()

        @pl.when(zs != z)
        def _():
            remote(zsend.at[zs, h], zin.at[zs, h], z_send.at[zs, h], z_recv.at[zs, h], me).wait_send()
    loop(0, nz * parts, sent_z)
    scaled_copy.wait()
    rows_copy.wait()


def finish(rows, scaled, token_in, router_in, weight_grad, token_grad, router_grad):
    weight_grad[0] = lax.dot_general(
        rows[0], scaled[...], (((0,), (0,)), ((), ())), preferred_element_type=F32).astype(BF16)
    token_grad[...] = token_in[...]
    router_grad[...] = router_in[...]


def local(tokens, logits, weights, router_weight, expert_picks, cotangent):
    n = lax.axis_size("expert")
    nz = 2 ** math.ceil(math.log2(n) / 3)
    parts = PARTS
    plane = n // nz
    tok, width = tokens.shape
    piece = width // parts
    cap = expert_picks.shape[1]
    hidden = weights.shape[2]
    most = max(2 * cap // n, 16)
    share = width // n
    rs_block = (n, share) if share % 128 == 0 else (share, n)
    rs_full = (n, width) if share % 128 == 0 else (width, n)
    vmem = pl.BlockSpec(memory_space=pltpu.VMEM)
    hbm = pl.BlockSpec(memory_space=pl.ANY)
    dma = pltpu.SemaphoreType.DMA
    flops = 2 * cap * width * hidden * 2
    token_in, rows, scaled, router_in = pl.pallas_call(
        functools.partial(kernel, n, nz, most, parts),
        out_shape=(
            jax.ShapeDtypeStruct((tok, width), BF16),
            jax.ShapeDtypeStruct((parts, cap, piece), BF16),
            jax.ShapeDtypeStruct((cap, hidden), BF16),
            jax.ShapeDtypeStruct(rs_block, F32),
        ),
        in_specs=[vmem, vmem, hbm, vmem, vmem, vmem],
        out_specs=(vmem, hbm, hbm, vmem),
        scratch_shapes=[
            pltpu.VMEM((width, hidden), BF16),
            pltpu.VMEM((n, tok), F32),
            pltpu.VMEM((n, 8, 128), F32),
            pltpu.VMEM((n, 8, 128), F32),
            pltpu.VMEM((nz, plane * most, tok), BF16),
            pltpu.VMEM((nz, tok, plane * most), BF16),
            pltpu.VMEM((cap, hidden), BF16),
            pltpu.VMEM((parts, cap, piece), BF16),
            pltpu.VMEM((nz, parts, tok, piece), BF16),
            pltpu.VMEM((nz, parts, plane * most, piece), BF16),
            pltpu.VMEM((parts, n * most, piece), BF16),
            pltpu.VMEM((nz, parts, plane * most, piece), BF16),
            pltpu.VMEM((nz, parts, plane * most, piece), BF16),
            pltpu.VMEM((nz + 1, parts, tok, piece), BF16),
            pltpu.VMEM((nz, parts, tok, piece), BF16),
            pltpu.VMEM((n, 8, 128), F32),
            pltpu.VMEM((n, 8, 128), F32),
            pltpu.VMEM(rs_full, F32),
            pltpu.VMEM((n,) + rs_block, F32),
            dma, dma((2,)),
            dma((n,)), dma((n,)),
            dma((2, nz, parts)), dma((nz, parts)),
            dma((nz, parts, plane)), dma((nz, parts, plane)),
            dma((nz, parts, plane)), dma((nz, parts, plane)),
            dma((nz, parts)), dma((nz + 1, parts)),
            dma((n,)), dma((n,)),
            dma((n,)), dma((n,)),
        ],
        compiler_params=pltpu.CompilerParams(
            collective_id=0, has_side_effects=True, vmem_limit_bytes=62 * 1024 * 1024),
        cost_estimate=pl.CostEstimate(flops=flops, bytes_accessed=8 * 2 ** 20, transcendentals=0),
    )(tokens, logits.T, weights, router_weight.T, expert_picks, cotangent[0])
    block = min(512, piece)
    per = piece // block
    weight_grad, token_grad, router_grad = pl.pallas_call(
        finish,
        grid=(width // block,),
        out_shape=(
            jax.ShapeDtypeStruct((1, width, hidden), BF16),
            jax.ShapeDtypeStruct((tok, width), BF16),
            jax.ShapeDtypeStruct(rs_block, F32),
        ),
        in_specs=[
            pl.BlockSpec((1, cap, block), lambda i: (i // per, 0, i % per)),
            pl.BlockSpec((cap, hidden), lambda i: (0, 0)),
            pl.BlockSpec((tok, block), lambda i: (0, i)),
            pl.BlockSpec(rs_block, lambda i: (0, 0)),
        ],
        out_specs=(
            pl.BlockSpec((1, block, hidden), lambda i: (0, i, 0)),
            pl.BlockSpec((tok, block), lambda i: (0, i)),
            pl.BlockSpec(rs_block, lambda i: (0, 0)),
        ),
        compiler_params=pltpu.CompilerParams(vmem_limit_bytes=62 * 1024 * 1024),
        cost_estimate=pl.CostEstimate(
            flops=flops // 2, bytes_accessed=7 * 2 ** 20, transcendentals=0),
    )(rows, scaled, token_in, router_in)
    return token_grad, weight_grad, router_grad.T if share % 128 == 0 else router_grad


def solution(mesh):
    in_specs = (
        P(("dp", "expert"), None),
        P(("dp", "expert"), None),
        P("expert", None, None),
        P(),
        P(("dp", "expert"), None),
        P(("dp", "expert"), None, None),
    )
    out_specs = (
        P(("dp", "expert"), None),
        P(("dp", "expert"), None, None),
        P(("dp", "expert"), None),
    )
    return jax.shard_map(local, mesh=mesh, in_specs=in_specs, out_specs=out_specs, check_vma=False)
```

```python
import functools
import math

import jax
import jax.numpy as jnp
from jax import lax
from jax.experimental import pallas as pl
from jax.experimental.pallas import tpu as pltpu
from jax.sharding import PartitionSpec as P

F32 = jnp.float32
BF16 = jnp.bfloat16
MESH = pl.DeviceIdType.MESH
PARTS = 2


def remote(src, dst, send, recv, peer):
    return pltpu.make_async_remote_copy(
        src_ref=src, dst_ref=dst, send_sem=send, recv_sem=recv,
        device_id={"expert": peer}, device_id_type=MESH)


def loop(low, high, body):
    def step(i, carry):
        body(i)
        return carry
    lax.fori_loop(low, high, step, 0)


def kernel(n, nz, most, parts,
           tokens, logits_t, weights, router_t, picks_ref, cot,
           token_grad, rows_out, scaled_out, router_grad,
           wbuf, probs, info_src, info_dst, sel, sel_t, scaled, rg,
           tokbuf, fwd_src, rowbuf, bwd_src, bwdbuf, zin, zsend,
           score_src, score_dst, rs_src, rs_dst,
           w_sem, out_sem, i_send, i_recv, a_send, a_recv, f_send, f_recv,
           b_send, b_recv, z_send, z_recv, s_send, s_recv, r_send, r_recv):
    plane = n // nz
    tok, width = tokens.shape
    piece = width // parts
    tile = min(512, piece)
    hidden = cot.shape[1]
    cap = cot.shape[0]
    me = lax.axis_index("expert")
    z = me // plane
    c = me % plane
    group = plane * most

    w_copy = pltpu.make_async_copy(weights.at[0], wbuf, w_sem)
    w_copy.start()
    barrier = pltpu.get_barrier_semaphore()
    loop(1, n, lambda i: pl.semaphore_signal(
        barrier, inc=1, device_id={"expert": lax.rem(me + i, n)}, device_id_type=MESH))

    scores = logits_t[...]
    exps = jnp.exp(scores - jnp.max(scores, axis=0, keepdims=True))
    probs[...] = exps / jnp.sum(exps, axis=0, keepdims=True)
    picks_row = picks_ref[...].astype(F32)
    info_src[...] = jnp.zeros_like(info_src)

    def fill_info(e):
        info_src[e, 0:1, :] = probs[pl.ds(e, 1), :]
        for k in range(cap // 128):
            info_src[e, 1 + k:2 + k, :] = picks_row[:, k * 128:(k + 1) * 128]
    loop(0, n, fill_info)
    info_dst[me] = info_src[me]
    for h in range(parts):
        tokbuf[z, h] = tokens[:, h * piece:(h + 1) * piece]

    picks_wide = jnp.concatenate(
        [jnp.broadcast_to(picks_row[:, k * 128:(k + 1) * 128], (128, 128)).T
         for k in range(cap // 128)], axis=0)
    picks_col = picks_wide[:, 0:1]

    def padded(values, other, axis, order):
        owner = jnp.floor(values * (1.0 / tok))
        before = jnp.sum(jnp.where(other < owner * tok, 1.0, 0.0), axis=axis, keepdims=True)
        return owner * most + order.astype(F32) - before
    placed_col = padded(picks_col, picks_row, 1, lax.broadcasted_iota(jnp.int32, (cap, 1), 0))
    placed_row = padded(picks_row, picks_col, 0, lax.broadcasted_iota(jnp.int32, (1, cap), 1))
    pl.semaphore_wait(barrier, n - 1)

    def info_copy(peer):
        return remote(info_src.at[peer], info_dst.at[me], i_send.at[peer], i_recv.at[me], peer)

    def info_arrival(peer):
        return remote(info_src.at[peer], info_dst.at[peer], i_send.at[peer], i_recv.at[peer], peer)

    loop(1, n, lambda i: info_copy(lax.rem(me + i, n)).start())

    def next_of(way):
        return me + plane * (1 - 2 * way)

    def goes_on(way):
        return jnp.where(way == 0, z < nz - 1, z > 0)

    def token_copy(way, src, h):
        return remote(tokbuf.at[src, h], tokbuf.at[src, h],
                      a_send.at[way, src, h], a_recv.at[src, h], next_of(way))

    def token_start(k):
        way, h = k % 2, k // 2

        @pl.when(goes_on(way))
        def _():
            token_copy(way, z, h).start()
    loop(0, 2 * parts, token_start)
    loop(1, n, lambda i: info_arrival(lax.rem(me + i, n)).wait_recv())

    def mine_of(c2):
        return pl.ds(pl.multiple_of(c2 * most, most), most)

    tok_col = lax.broadcasted_iota(jnp.int32, (tok, 128), 0).astype(F32)
    slot_lane = lax.broadcasted_iota(jnp.int32, (tok, group), 1).astype(F32)

    def build_sel(zs):
        base = ((zs * plane + c) * tok).astype(F32)

        def one(e, acc):
            rank = jnp.zeros((tok, 128), F32)
            member = jnp.zeros((tok, 128), F32)
            for k in range(cap // 128):
                rel = info_dst[z * plane + e, 1 + k:2 + k, :] - base
                rank += jnp.where((rel >= 0.0) & (rel < tok_col), 1.0, 0.0)
                member += jnp.where(rel == tok_col, 1.0, 0.0)
            rank = jnp.sum(rank, axis=1, keepdims=True)
            member = jnp.sum(member, axis=1, keepdims=True)
            first = (e * most).astype(F32)
            return acc + jnp.where(slot_lane == rank + first, member, 0.0)

        made = lax.fori_loop(0, plane, one, jnp.zeros((tok, group), F32))
        sel_t[zs] = made.astype(BF16)
        sel[zs] = made.T.astype(BF16)

    def rows_of(zs, c2):
        return pl.ds(pl.multiple_of((zs * plane + c2) * most, most), most)

    def fwd_copy(zs, h, c2):
        return remote(fwd_src.at[zs, h, mine_of(c2), :], rowbuf.at[h, rows_of(zs, c), :],
                      f_send.at[zs, h, c2], f_recv.at[zs, h, c], z * plane + c2)

    def fwd_arrival(zs, h, c2):
        return remote(fwd_src.at[zs, h, mine_of(c2), :], rowbuf.at[h, rows_of(zs, c2), :],
                      f_send.at[zs, h, c2], f_recv.at[zs, h, c2], z * plane + c2)

    def pick_rows(src, h):
        for t in range(piece // tile):
            lanes = slice(t * tile, (t + 1) * tile)
            fwd_src[src, h, :, lanes] = jnp.dot(
                sel[src], tokbuf[src, h, :, lanes], preferred_element_type=F32).astype(BF16)
        loop(1, plane, lambda i: fwd_copy(src, h, lax.rem(c + i, plane)).start())
        rowbuf[h, rows_of(src, c), :] = fwd_src[src, h, mine_of(c), :]

    build_sel(z)
    loop(0, parts, lambda h: pick_rows(z, h))

    lane = lax.broadcasted_iota(jnp.int32, (cap, 128), 1).astype(F32)

    def add_gate(o, acc):
        hit = (picks_col - (o * tok).astype(F32)) == lane
        return acc + jnp.where(hit, info_dst[o, 0:1, :], 0.0)
    gate = jnp.sum(lax.fori_loop(0, n, add_gate, jnp.zeros((cap, 128), F32)), axis=1, keepdims=True)
    gate = gate.astype(BF16).astype(F32)
    scaled[...] = (gate * cot[...].astype(F32)).astype(BF16)
    scaled_copy = pltpu.make_async_copy(scaled, scaled_out, out_sem.at[0])
    scaled_copy.start()
    w_copy.wait()

    def row_tile(t):
        rows = pl.ds(pl.multiple_of(t * tile, tile), tile)
        per = piece // tile
        lanes = pl.ds(pl.multiple_of((t % per) * tile, tile), tile)
        rg[t // per, :, lanes] = lax.dot_general(
            scaled[...], wbuf[rows, :], (((1,), (1,)), ((), ())),
            preferred_element_type=F32).astype(BF16)
    loop(0, width // tile, row_tile)

    def bwd_copy(zd, h, c2):
        return remote(bwd_src.at[zd, h, mine_of(c2), :], bwdbuf.at[zd, h, mine_of(c), :],
                      b_send.at[zd, h, c2], b_recv.at[zd, h, c], z * plane + c2)

    def bwd_arrival(zd, h, c2):
        return remote(bwd_src.at[zd, h, mine_of(c2), :], bwdbuf.at[zd, h, mine_of(c2), :],
                      b_send.at[zd, h, c2], b_recv.at[zd, h, c2], z * plane + c2)

    slot_row = lax.broadcasted_iota(jnp.int32, (group, cap), 0).astype(F32)

    def backward(zd, h):
        low = (zd * group).astype(F32)
        spread = jnp.where(slot_row == placed_row - low, 1.0, 0.0).astype(BF16)
        for t in range(piece // tile):
            lanes = slice(t * tile, (t + 1) * tile)
            bwd_src[zd, h, :, lanes] = jnp.dot(
                spread, rg[h, :, lanes], preferred_element_type=F32).astype(BF16)
        loop(1, plane, lambda i: bwd_copy(zd, h, lax.rem(c + i, plane)).start())
        bwdbuf[zd, h, mine_of(c), :] = bwd_src[zd, h, mine_of(c), :]

    def chain_place(q, way):
        start = jnp.where(way == 0, z, nz - 1 - z)
        k = q - start
        block = jnp.maximum(k, 0) // parts
        dest = jnp.where(way == 0, nz - 1 - block, block)
        valid = (k >= 0) & (block < nz - 1 - start)
        return valid, jnp.minimum(jnp.maximum(dest, 0), nz - 1), jnp.maximum(k, 0) % parts, start > 0

    def backward_at(q):
        def one(way):
            valid, dest, h, _ = chain_place(q, way)

            @pl.when(valid)
            def _():
                backward(dest, h)
        loop(0, 2, one)

    late = parts + 1
    loop(0, parts, backward_at)

    loop(1, nz, lambda k: build_sel(lax.rem(z + k, nz)))

    def forward_at(q, way):
        far, h = q // parts, q % parts
        src = z + (2 * way - 1) * far

        @pl.when((src >= 0) & (src < nz) & (far > 0))
        def _():
            token_copy(way, src, h).wait_recv()

            @pl.when(goes_on(way))
            def _():
                token_copy(way, src, h).start()
            pick_rows(src, h)

    def chain_at(q, way):
        valid, dest, h, has_in = chain_place(q, way)
        out_slot = jnp.where((way == 1) & (dest == z - 1), nz, dest)

        @pl.when(valid)
        def _():
            loop(1, plane, lambda i: bwd_arrival(dest, h, lax.rem(c + i, plane)).wait_recv())

            @pl.when(has_in)
            def _():
                remote(zsend.at[dest, h], zin.at[dest, h], z_send.at[dest, h],
                       z_recv.at[dest, h], me).wait_recv()

            @pl.when(jnp.logical_not(has_in))
            def _():
                zin[dest, h] = jnp.zeros(zin.shape[2:], BF16)
            for t in range(piece // tile):
                lanes = slice(t * tile, (t + 1) * tile)
                zsend[dest, h, :, lanes] = (jnp.dot(
                    sel_t[dest], bwdbuf[dest, h, :, lanes], preferred_element_type=F32)
                    + zin[dest, h, :, lanes].astype(F32)).astype(BF16)
            remote(zsend.at[dest, h], zin.at[out_slot, h], z_send.at[dest, h],
                   z_recv.at[out_slot, h], next_of(way)).start()

    def substep(q):
        loop(0, 2, lambda way: forward_at(q, way))

        @pl.when(q >= parts)
        def _():
            backward_at(q)


        @pl.when((q >= parts * nz - 1) & (q < parts * nz + parts - 1))
        def _():
            backward(z, q - (parts * nz - 1))
        loop(0, 2, lambda way: chain_at(q - late, way))
    loop(0, nz * parts + late, substep)

    slot_lanes = lax.broadcasted_iota(jnp.int32, (cap, n * most), 1).astype(F32)
    compact = jnp.where(slot_lanes == placed_col, 1.0, 0.0).astype(BF16)
    rc = rg

    def gate_part(h, total):
        def rows_arrived(k):
            zs = k // plane
            c2 = k % plane

            @pl.when(c2 != c)
            def _():
                fwd_arrival(zs, h, c2).wait_recv()
        loop(0, n, rows_arrived)
        for t in range(piece // tile):
            lanes = slice(t * tile, (t + 1) * tile)
            rc[h, :, lanes] = jnp.dot(
                compact, rowbuf[h, :, lanes], preferred_element_type=F32).astype(BF16)

        def active_tile(t, acc):
            lanes = pl.ds(pl.multiple_of(t * 256, 256), 256)
            depth = pl.ds(pl.multiple_of(h * piece, piece), piece)
            active = jnp.dot(rc[h], wbuf[depth, lanes], preferred_element_type=F32)
            return acc + jnp.sum(cot[:, lanes].astype(F32) * active, axis=1, keepdims=True)
        return lax.fori_loop(0, hidden // 256, active_tile, total)
    gate_grad = lax.fori_loop(0, parts, gate_part, jnp.zeros((cap, 1), F32))
    gate_grad = gate_grad.astype(BF16).astype(F32)
    rows_copy = pltpu.make_async_copy(rc, rows_out, out_sem.at[1])
    rows_copy.start()

    def score_copy(peer):
        return remote(score_src.at[peer], score_dst.at[me], s_send.at[peer], s_recv.at[me], peer)

    def score_arrival(peer):
        return remote(score_src.at[peer], score_dst.at[peer], s_send.at[peer], s_recv.at[peer], peer)

    score_src[...] = jnp.zeros_like(score_src)

    def score_row(i):
        o = lax.rem(me + i, n)
        hit = (picks_col - (o * tok).astype(F32)) == lane
        score_src[o, 0:1, :] = jnp.sum(jnp.where(hit, gate_grad, 0.0), axis=0, keepdims=True)

    def score_send(i):
        score_row(i)
        score_copy(lax.rem(me + i, n)).start()
    loop(1, n, score_send)
    score_row(0)
    score_dst[me] = score_src[me]

    def own_back(h):
        loop(1, plane, lambda i: bwd_arrival(z, h, lax.rem(c + i, plane)).wait_recv())

        @pl.when(z == 0)
        def _():
            zin[z, h] = jnp.zeros(zin.shape[2:], BF16)

        @pl.when(z == nz - 1)
        def _():
            zin[nz, h] = jnp.zeros(zin.shape[2:], BF16)

        @pl.when(z > 0)
        def _():
            remote(zsend.at[z, h], zin.at[z, h], z_send.at[z, h], z_recv.at[z, h], me).wait_recv()

        @pl.when(z < nz - 1)
        def _():
            remote(zsend.at[z, h], zin.at[nz, h], z_send.at[z, h], z_recv.at[nz, h], me).wait_recv()
    loop(1, n, lambda i: score_arrival(lax.rem(me + i, n)).wait_recv())
    score = score_dst[:, 0, :]
    prob = probs[...]
    inner = jnp.sum(prob * score, axis=0, keepdims=True)
    logit_grad = prob * (score - inner)
    logit_col = logit_grad.T.astype(BF16)
    logit_grad = logit_grad.astype(BF16)
    share = width // n
    wide = share % 128 == 0

    def router_tile(t):
        lanes = pl.ds(pl.multiple_of(t * 512, 512), 512)
        part = jnp.dot(logit_grad, tokens[:, lanes], preferred_element_type=F32)
        if wide:
            rs_src[:, lanes] = part
        else:
            rs_src[lanes, :] = part.T
    loop(0, width // 512, router_tile)

    def share_of(d):
        if wide:
            return rs_src.at[:, pl.ds(pl.multiple_of(d * share, share), share)]
        return rs_src.at[pl.ds(pl.multiple_of(d * share, share), share), :]

    def rs_copy(peer):
        return remote(share_of(peer), rs_dst.at[me], r_send.at[peer], r_recv.at[me], peer)

    def rs_arrival(peer):
        return remote(share_of(peer), rs_dst.at[peer], r_send.at[peer], r_recv.at[peer], peer)
    loop(1, n, lambda i: rs_copy(lax.rem(me + i, n)).start())
    rs_dst[me] = share_of(me)[...]

    def final_part(h):
        own_back(h)
        for t in range(piece // tile):
            lanes = slice(t * tile, (t + 1) * tile)
            whole = pl.ds(pl.multiple_of(h * piece + t * tile, tile), tile)
            total = jnp.dot(sel_t[z], bwdbuf[z, h, :, lanes], preferred_element_type=F32)
            total += zin[z, h, :, lanes].astype(F32) + zin[nz, h, :, lanes].astype(F32)
            total += jnp.dot(logit_col, router_t[:, whole], preferred_element_type=F32)
            token_grad[:, whole] = total.astype(BF16)
    loop(0, parts, final_part)

    loop(1, n, lambda i: rs_arrival(lax.rem(me + i, n)).wait_recv())
    total = jnp.sum(rs_dst[...], axis=0)
    router_grad[...] = total

    def sent(i):
        peer = lax.rem(me + i, n)
        info_copy(peer).wait_send()
        score_copy(peer).wait_send()
        rs_copy(peer).wait_send()
    loop(1, n, sent)

    def sent_plane(k):
        zs = k // (plane * parts)
        h = (k // plane) % parts
        c2 = k % plane

        @pl.when(c2 != c)
        def _():
            fwd_copy(zs, h, c2).wait_send()
            bwd_copy(zs, h, c2).wait_send()
    loop(0, n * parts, sent_plane)

    def sent_z(k):
        zs, h = k // parts, k % parts

        @pl.when((z < nz - 1) & (zs <= z))
        def _():
            token_copy(0, zs, h).wait_send()

        @pl.when((z > 0) & (zs >= z))
        def _():
            token_copy(1, zs, h).wait_send()

        @pl.when(zs != z)
        def _():
            remote(zsend.at[zs, h], zin.at[zs, h], z_send.at[zs, h], z_recv.at[zs, h], me).wait_send()
    loop(0, nz * parts, sent_z)
    scaled_copy.wait()
    rows_copy.wait()


def finish(rows, scaled, token_in, router_in, weight_grad, token_grad, router_grad):
    weight_grad[0] = lax.dot_general(
        rows[0], scaled[...], (((0,), (0,)), ((), ())), preferred_element_type=F32).astype(BF16)
    token_grad[...] = token_in[...]
    router_grad[...] = router_in[...]


def local(tokens, logits, weights, router_weight, expert_picks, cotangent):
    n = lax.axis_size("expert")
    nz = 2 ** math.ceil(math.log2(n) / 3)
    parts = PARTS
    plane = n // nz
    tok, width = tokens.shape
    piece = width // parts
    cap = expert_picks.shape[1]
    hidden = weights.shape[2]
    most = max(2 * cap // n, 16)
    share = width // n
    rs_block = (n, share) if share % 128 == 0 else (share, n)
    rs_full = (n, width) if share % 128 == 0 else (width, n)
    vmem = pl.BlockSpec(memory_space=pltpu.VMEM)
    hbm = pl.BlockSpec(memory_space=pl.ANY)
    dma = pltpu.SemaphoreType.DMA
    flops = 2 * cap * width * hidden * 2
    token_in, rows, scaled, router_in = pl.pallas_call(
        functools.partial(kernel, n, nz, most, parts),
        out_shape=(
            jax.ShapeDtypeStruct((tok, width), BF16),
            jax.ShapeDtypeStruct((parts, cap, piece), BF16),
            jax.ShapeDtypeStruct((cap, hidden), BF16),
            jax.ShapeDtypeStruct(rs_block, F32),
        ),
        in_specs=[vmem, vmem, hbm, vmem, vmem, vmem],
        out_specs=(vmem, hbm, hbm, vmem),
        scratch_shapes=[
            pltpu.VMEM((width, hidden), BF16),
            pltpu.VMEM((n, tok), F32),
            pltpu.VMEM((n, 8, 128), F32),
            pltpu.VMEM((n, 8, 128), F32),
            pltpu.VMEM((nz, plane * most, tok), BF16),
            pltpu.VMEM((nz, tok, plane * most), BF16),
            pltpu.VMEM((cap, hidden), BF16),
            pltpu.VMEM((parts, cap, piece), BF16),
            pltpu.VMEM((nz, parts, tok, piece), BF16),
            pltpu.VMEM((nz, parts, plane * most, piece), BF16),
            pltpu.VMEM((parts, n * most, piece), BF16),
            pltpu.VMEM((nz, parts, plane * most, piece), BF16),
            pltpu.VMEM((nz, parts, plane * most, piece), BF16),
            pltpu.VMEM((nz + 1, parts, tok, piece), BF16),
            pltpu.VMEM((nz, parts, tok, piece), BF16),
            pltpu.VMEM((n, 8, 128), F32),
            pltpu.VMEM((n, 8, 128), F32),
            pltpu.VMEM(rs_full, F32),
            pltpu.VMEM((n,) + rs_block, F32),
            dma, dma((2,)),
            dma((n,)), dma((n,)),
            dma((2, nz, parts)), dma((nz, parts)),
            dma((nz, parts, plane)), dma((nz, parts, plane)),
            dma((nz, parts, plane)), dma((nz, parts, plane)),
            dma((nz, parts)), dma((nz + 1, parts)),
            dma((n,)), dma((n,)),
            dma((n,)), dma((n,)),
        ],
        compiler_params=pltpu.CompilerParams(
            collective_id=0, has_side_effects=True, vmem_limit_bytes=62 * 1024 * 1024),
        cost_estimate=pl.CostEstimate(flops=flops, bytes_accessed=8 * 2 ** 20, transcendentals=0),
    )(tokens, logits.T, weights, router_weight.T, expert_picks, cotangent[0])
    block = min(512, piece)
    per = piece // block
    weight_grad, token_grad, router_grad = pl.pallas_call(
        finish,
        grid=(width // block,),
        out_shape=(
            jax.ShapeDtypeStruct((1, width, hidden), BF16),
            jax.ShapeDtypeStruct((tok, width), BF16),
            jax.ShapeDtypeStruct(rs_block, F32),
        ),
        in_specs=[
            pl.BlockSpec((1, cap, block), lambda i: (i // per, 0, i % per)),
            pl.BlockSpec((cap, hidden), lambda i: (0, 0)),
            pl.BlockSpec((tok, block), lambda i: (0, i)),
            pl.BlockSpec(rs_block, lambda i: (0, 0)),
        ],
        out_specs=(
            pl.BlockSpec((1, block, hidden), lambda i: (0, i, 0)),
            pl.BlockSpec((tok, block), lambda i: (0, i)),
            pl.BlockSpec(rs_block, lambda i: (0, 0)),
        ),
        compiler_params=pltpu.CompilerParams(vmem_limit_bytes=62 * 1024 * 1024),
        cost_estimate=pl.CostEstimate(
            flops=flops // 2, bytes_accessed=7 * 2 ** 20, transcendentals=0),
    )(rows, scaled, token_in, router_in)
    return token_grad, weight_grad, router_grad.T if share % 128 == 0 else router_grad


def solution(mesh):
    in_specs = (
        P(("dp", "expert"), None),
        P(("dp", "expert"), None),
        P("expert", None, None),
        P(),
        P(("dp", "expert"), None),
        P(("dp", "expert"), None, None),
    )
    out_specs = (
        P(("dp", "expert"), None),
        P(("dp", "expert"), None, None),
        P(("dp", "expert"), None),
    )
    return jax.shard_map(local, mesh=mesh, in_specs=in_specs, out_specs=out_specs, check_vma=False)
```

```python
import functools
import math

import jax
import jax.numpy as jnp
from jax import lax
from jax.experimental import pallas as pl
from jax.experimental.pallas import tpu as pltpu
from jax.sharding import PartitionSpec as P

F32 = jnp.float32
BF16 = jnp.bfloat16
MESH = pl.DeviceIdType.MESH
PARTS = 2


def remote(src, dst, send, recv, peer):
    return pltpu.make_async_remote_copy(
        src_ref=src, dst_ref=dst, send_sem=send, recv_sem=recv,
        device_id={"expert": peer}, device_id_type=MESH)


def loop(low, high, body):
    def step(i, carry):
        body(i)
        return carry
    lax.fori_loop(low, high, step, 0)


def kernel(n, nz, most, parts,
           tokens, logits_t, weights, router_t, picks_ref, cot,
           token_grad, rows_out, scaled_out, router_grad,
           wbuf, probs, info_src, info_dst, sel, sel_t, scaled, rg,
           tokbuf, fwd_src, rowbuf, bwd_src, bwdbuf, zin, zsend,
           score_src, score_dst, rs_src, rs_dst,
           w_sem, out_sem, i_send, i_recv, a_send, a_recv, f_send, f_recv,
           b_send, b_recv, z_send, z_recv, s_send, s_recv, r_send, r_recv):
    plane = n // nz
    tok, width = tokens.shape
    piece = width // parts
    tile = min(512, piece)
    hidden = cot.shape[1]
    cap = cot.shape[0]
    me = lax.axis_index("expert")
    z = me // plane
    c = me % plane
    group = plane * most

    w_copy = pltpu.make_async_copy(weights.at[0], wbuf, w_sem)
    w_copy.start()
    barrier = pltpu.get_barrier_semaphore()
    loop(1, n, lambda i: pl.semaphore_signal(
        barrier, inc=1, device_id={"expert": lax.rem(me + i, n)}, device_id_type=MESH))

    scores = logits_t[...]
    exps = jnp.exp(scores - jnp.max(scores, axis=0, keepdims=True))
    probs[...] = exps / jnp.sum(exps, axis=0, keepdims=True)
    picks_row = picks_ref[...].astype(F32)
    info_src[...] = jnp.zeros_like(info_src)

    def fill_info(e):
        info_src[e, 0:1, :] = probs[pl.ds(e, 1), :]
        for k in range(cap // 128):
            info_src[e, 1 + k:2 + k, :] = picks_row[:, k * 128:(k + 1) * 128]
    loop(0, n, fill_info)
    info_dst[me] = info_src[me]
    for h in range(parts):
        tokbuf[z, h] = tokens[:, h * piece:(h + 1) * piece]

    picks_wide = jnp.concatenate(
        [jnp.broadcast_to(picks_row[:, k * 128:(k + 1) * 128], (128, 128)).T
         for k in range(cap // 128)], axis=0)
    picks_col = picks_wide[:, 0:1]

    def padded(values, other, axis, order):
        owner = jnp.floor(values * (1.0 / tok))
        before = jnp.sum(jnp.where(other < owner * tok, 1.0, 0.0), axis=axis, keepdims=True)
        return owner * most + order.astype(F32) - before
    placed_col = padded(picks_col, picks_row, 1, lax.broadcasted_iota(jnp.int32, (cap, 1), 0))
    placed_row = padded(picks_row, picks_col, 0, lax.broadcasted_iota(jnp.int32, (1, cap), 1))
    pl.semaphore_wait(barrier, n - 1)

    def info_copy(peer):
        return remote(info_src.at[peer], info_dst.at[me], i_send.at[peer], i_recv.at[me], peer)

    def info_arrival(peer):
        return remote(info_src.at[peer], info_dst.at[peer], i_send.at[peer], i_recv.at[peer], peer)

    loop(1, n, lambda i: info_copy(lax.rem(me + i, n)).start())

    def next_of(way):
        return lax.rem(me + plane * (1 - 2 * way) + n, n)

    def goes_on(way):
        return jnp.where(way == 0, z < nz - 1, z > 0)

    def token_copy(way, src, h):
        return remote(tokbuf.at[src, h], tokbuf.at[src, h],
                      a_send.at[way, src, h], a_recv.at[src, h], next_of(way))

    def token_start(k):
        way, h = k % 2, k // 2

        @pl.when(goes_on(way))
        def _():
            token_copy(way, z, h).start()
    loop(0, 2 * parts, token_start)
    loop(1, n, lambda i: info_arrival(lax.rem(me + i, n)).wait_recv())

    def mine_of(c2):
        return pl.ds(pl.multiple_of(c2 * most, most), most)

    tok_col = lax.broadcasted_iota(jnp.int32, (tok, 128), 0).astype(F32)
    slot_lane = lax.broadcasted_iota(jnp.int32, (tok, group), 1).astype(F32)

    def build_sel(zs):
        base = ((zs * plane + c) * tok).astype(F32)

        def one(e, acc):
            rank = jnp.zeros((tok, 128), F32)
            member = jnp.zeros((tok, 128), F32)
            for k in range(cap // 128):
                rel = info_dst[z * plane + e, 1 + k:2 + k, :] - base
                rank += jnp.where((rel >= 0.0) & (rel < tok_col), 1.0, 0.0)
                member += jnp.where(rel == tok_col, 1.0, 0.0)
            rank = jnp.sum(rank, axis=1, keepdims=True)
            member = jnp.sum(member, axis=1, keepdims=True)
            first = (e * most).astype(F32)
            return acc + jnp.where(slot_lane == rank + first, member, 0.0)

        made = lax.fori_loop(0, plane, one, jnp.zeros((tok, group), F32))
        sel_t[zs] = made.astype(BF16)
        sel[zs] = made.T.astype(BF16)

    def rows_of(zs, c2):
        return pl.ds(pl.multiple_of((zs * plane + c2) * most, most), most)

    def fwd_copy(zs, h, c2):
        return remote(fwd_src.at[zs, h, mine_of(c2), :], rowbuf.at[h, rows_of(zs, c), :],
                      f_send.at[zs, h, c2], f_recv.at[zs, h, c], z * plane + c2)

    def fwd_arrival(zs, h, c2):
        return remote(fwd_src.at[zs, h, mine_of(c2), :], rowbuf.at[h, rows_of(zs, c2), :],
                      f_send.at[zs, h, c2], f_recv.at[zs, h, c2], z * plane + c2)

    def pick_rows(src, h):
        for t in range(piece // tile):
            lanes = slice(t * tile, (t + 1) * tile)
            fwd_src[src, h, :, lanes] = jnp.dot(
                sel[src], tokbuf[src, h, :, lanes], preferred_element_type=F32).astype(BF16)
        loop(1, plane, lambda i: fwd_copy(src, h, lax.rem(c + i, plane)).start())
        rowbuf[h, rows_of(src, c), :] = fwd_src[src, h, mine_of(c), :]

    build_sel(z)
    loop(0, parts, lambda h: pick_rows(z, h))

    lane = lax.broadcasted_iota(jnp.int32, (cap, 128), 1).astype(F32)

    def add_gate(o, acc):
        hit = (picks_col - (o * tok).astype(F32)) == lane
        return acc + jnp.where(hit, info_dst[o, 0:1, :], 0.0)
    gate = jnp.sum(lax.fori_loop(0, n, add_gate, jnp.zeros((cap, 128), F32)), axis=1, keepdims=True)
    gate = gate.astype(BF16).astype(F32)
    scaled[...] = (gate * cot[...].astype(F32)).astype(BF16)
    scaled_copy = pltpu.make_async_copy(scaled, scaled_out, out_sem.at[0])
    scaled_copy.start()
    w_copy.wait()

    def row_tile(t):
        rows = pl.ds(pl.multiple_of(t * tile, tile), tile)
        per = piece // tile
        lanes = pl.ds(pl.multiple_of((t % per) * tile, tile), tile)
        rg[t // per, :, lanes] = lax.dot_general(
            scaled[...], wbuf[rows, :], (((1,), (1,)), ((), ())),
            preferred_element_type=F32).astype(BF16)
    loop(0, width // tile, row_tile)

    def bwd_copy(zd, h, c2):
        return remote(bwd_src.at[zd, h, mine_of(c2), :], bwdbuf.at[zd, h, mine_of(c), :],
                      b_send.at[zd, h, c2], b_recv.at[zd, h, c], z * plane + c2)

    def bwd_arrival(zd, h, c2):
        return remote(bwd_src.at[zd, h, mine_of(c2), :], bwdbuf.at[zd, h, mine_of(c2), :],
                      b_send.at[zd, h, c2], b_recv.at[zd, h, c2], z * plane + c2)

    slot_row = lax.broadcasted_iota(jnp.int32, (group, cap), 0).astype(F32)

    def backward(zd, h):
        low = (zd * group).astype(F32)
        spread = jnp.where(slot_row == placed_row - low, 1.0, 0.0).astype(BF16)
        for t in range(piece // tile):
            lanes = slice(t * tile, (t + 1) * tile)
            bwd_src[zd, h, :, lanes] = jnp.dot(
                spread, rg[h, :, lanes], preferred_element_type=F32).astype(BF16)
        loop(1, plane, lambda i: bwd_copy(zd, h, lax.rem(c + i, plane)).start())
        bwdbuf[zd, h, mine_of(c), :] = bwd_src[zd, h, mine_of(c), :]

    def chain_place(q, way):
        start = jnp.where(way == 0, z, nz - 1 - z)
        k = q - start
        block = jnp.maximum(k, 0) // parts
        dest = jnp.where(way == 0, nz - 1 - block, block)
        valid = (k >= 0) & (block < nz - 1 - start)
        return valid, jnp.minimum(jnp.maximum(dest, 0), nz - 1), jnp.maximum(k, 0) % parts, start > 0

    def backward_at(q):
        def one(way):
            valid, dest, h, _ = chain_place(q, way)

            @pl.when(valid)
            def _():
                backward(dest, h)
        loop(0, 2, one)

    late = parts + 1
    loop(0, parts, backward_at)

    loop(1, nz, lambda k: build_sel(lax.rem(z + k, nz)))

    def forward_at(q, way):
        far, h = q // parts, q % parts
        src = z + (2 * way - 1) * far

        @pl.when((src >= 0) & (src < nz) & (far > 0))
        def _():
            token_copy(way, src, h).wait_recv()

            @pl.when(goes_on(way))
            def _():
                token_copy(way, src, h).start()
            pick_rows(src, h)

    def chain_at(q, way):
        valid, dest, h, has_in = chain_place(q, way)
        out_slot = jnp.where((way == 1) & (dest == z - 1), nz, dest)

        @pl.when(valid)
        def _():
            loop(1, plane, lambda i: bwd_arrival(dest, h, lax.rem(c + i, plane)).wait_recv())

            @pl.when(has_in)
            def _():
                remote(zsend.at[dest, h], zin.at[dest, h], z_send.at[dest, h],
                       z_recv.at[dest, h], me).wait_recv()

            @pl.when(jnp.logical_not(has_in))
            def _():
                zin[dest, h] = jnp.zeros(zin.shape[2:], BF16)
            for t in range(piece // tile):
                lanes = slice(t * tile, (t + 1) * tile)
                zsend[dest, h, :, lanes] = (jnp.dot(
                    sel_t[dest], bwdbuf[dest, h, :, lanes], preferred_element_type=F32)
                    + zin[dest, h, :, lanes].astype(F32)).astype(BF16)
            remote(zsend.at[dest, h], zin.at[out_slot, h], z_send.at[dest, h],
                   z_recv.at[out_slot, h], next_of(way)).start()

    def substep(q):
        loop(0, 2, lambda way: forward_at(q, way))

        @pl.when(q >= parts)
        def _():
            backward_at(q)


        @pl.when((q >= parts * nz - 1) & (q < parts * nz + parts - 1))
        def _():
            backward(z, q - (parts * nz - 1))
        loop(0, 2, lambda way: chain_at(q - late, way))
    loop(0, nz * parts + late, substep)

    slot_lanes = lax.broadcasted_iota(jnp.int32, (cap, n * most), 1).astype(F32)
    compact = jnp.where(slot_lanes == placed_col, 1.0, 0.0).astype(BF16)
    rc = rg

    def gate_part(h, total):
        def rows_arrived(k):
            zs = k // plane
            c2 = k % plane

            @pl.when(c2 != c)
            def _():
                fwd_arrival(zs, h, c2).wait_recv()
        loop(0, n, rows_arrived)
        for t in range(piece // tile):
            lanes = slice(t * tile, (t + 1) * tile)
            rc[h, :, lanes] = jnp.dot(
                compact, rowbuf[h, :, lanes], preferred_element_type=F32).astype(BF16)

        def active_tile(t, acc):
            lanes = pl.ds(pl.multiple_of(t * 256, 256), 256)
            depth = pl.ds(pl.multiple_of(h * piece, piece), piece)
            active = jnp.dot(rc[h], wbuf[depth, lanes], preferred_element_type=F32)
            return acc + jnp.sum(cot[:, lanes].astype(F32) * active, axis=1, keepdims=True)
        return lax.fori_loop(0, hidden // 256, active_tile, total)
    gate_grad = lax.fori_loop(0, parts, gate_part, jnp.zeros((cap, 1), F32))
    gate_grad = gate_grad.astype(BF16).astype(F32)
    rows_copy = pltpu.make_async_copy(rc, rows_out, out_sem.at[1])
    rows_copy.start()

    def score_copy(peer):
        return remote(score_src.at[peer], score_dst.at[me], s_send.at[peer], s_recv.at[me], peer)

    def score_arrival(peer):
        return remote(score_src.at[peer], score_dst.at[peer], s_send.at[peer], s_recv.at[peer], peer)

    score_src[...] = jnp.zeros_like(score_src)

    def score_row(i):
        o = lax.rem(me + i, n)
        hit = (picks_col - (o * tok).astype(F32)) == lane
        score_src[o, 0:1, :] = jnp.sum(jnp.where(hit, gate_grad, 0.0), axis=0, keepdims=True)

    def score_send(i):
        score_row(i)
        score_copy(lax.rem(me + i, n)).start()
    loop(1, n, score_send)
    score_row(0)
    score_dst[me] = score_src[me]

    def own_back(h):
        loop(1, plane, lambda i: bwd_arrival(z, h, lax.rem(c + i, plane)).wait_recv())

        @pl.when(z == 0)
        def _():
            zin[z, h] = jnp.zeros(zin.shape[2:], BF16)

        @pl.when(z == nz - 1)
        def _():
            zin[nz, h] = jnp.zeros(zin.shape[2:], BF16)

        @pl.when(z > 0)
        def _():
            remote(zsend.at[z, h], zin.at[z, h], z_send.at[z, h], z_recv.at[z, h], me).wait_recv()

        @pl.when(z < nz - 1)
        def _():
            remote(zsend.at[z, h], zin.at[nz, h], z_send.at[z, h], z_recv.at[nz, h], me).wait_recv()
    loop(1, n, lambda i: score_arrival(lax.rem(me + i, n)).wait_recv())
    score = score_dst[:, 0, :]
    prob = probs[...]
    inner = jnp.sum(prob * score, axis=0, keepdims=True)
    logit_grad = prob * (score - inner)
    logit_col = logit_grad.T.astype(BF16)
    logit_grad = logit_grad.astype(BF16)
    share = width // n
    wide = share % 128 == 0

    def router_tile(t):
        lanes = pl.ds(pl.multiple_of(t * 512, 512), 512)
        part = jnp.dot(logit_grad, tokens[:, lanes], preferred_element_type=F32)
        if wide:
            rs_src[:, lanes] = part
        else:
            rs_src[lanes, :] = part.T
    loop(0, width // 512, router_tile)

    def share_of(d):
        if wide:
            return rs_src.at[:, pl.ds(pl.multiple_of(d * share, share), share)]
        return rs_src.at[pl.ds(pl.multiple_of(d * share, share), share), :]

    def rs_copy(peer):
        return remote(share_of(peer), rs_dst.at[me], r_send.at[peer], r_recv.at[me], peer)

    def rs_arrival(peer):
        return remote(share_of(peer), rs_dst.at[peer], r_send.at[peer], r_recv.at[peer], peer)
    loop(1, n, lambda i: rs_copy(lax.rem(me + i, n)).start())
    rs_dst[me] = share_of(me)[...]

    def final_part(h):
        own_back(h)
        for t in range(piece // tile):
            lanes = slice(t * tile, (t + 1) * tile)
            whole = pl.ds(pl.multiple_of(h * piece + t * tile, tile), tile)
            total = jnp.dot(sel_t[z], bwdbuf[z, h, :, lanes], preferred_element_type=F32)
            total += zin[z, h, :, lanes].astype(F32) + zin[nz, h, :, lanes].astype(F32)
            total += jnp.dot(logit_col, router_t[:, whole], preferred_element_type=F32)
            token_grad[:, whole] = total.astype(BF16)
    loop(0, parts, final_part)

    loop(1, n, lambda i: rs_arrival(lax.rem(me + i, n)).wait_recv())
    total = jnp.sum(rs_dst[...], axis=0)
    router_grad[...] = total

    def sent(i):
        peer = lax.rem(me + i, n)
        info_copy(peer).wait_send()
        score_copy(peer).wait_send()
        rs_copy(peer).wait_send()
    loop(1, n, sent)

    def sent_plane(k):
        zs = k // (plane * parts)
        h = (k // plane) % parts
        c2 = k % plane

        @pl.when(c2 != c)
        def _():
            fwd_copy(zs, h, c2).wait_send()
            bwd_copy(zs, h, c2).wait_send()
    loop(0, n * parts, sent_plane)

    def sent_z(k):
        zs, h = k // parts, k % parts

        @pl.when((z < nz - 1) & (zs <= z))
        def _():
            token_copy(0, zs, h).wait_send()

        @pl.when((z > 0) & (zs >= z))
        def _():
            token_copy(1, zs, h).wait_send()

        @pl.when(zs != z)
        def _():
            remote(zsend.at[zs, h], zin.at[zs, h], z_send.at[zs, h], z_recv.at[zs, h], me).wait_send()
    loop(0, nz * parts, sent_z)
    scaled_copy.wait()
    rows_copy.wait()


def finish(rows, scaled, token_in, router_in, weight_grad, token_grad, router_grad):
    weight_grad[0] = lax.dot_general(
        rows[0], scaled[...], (((0,), (0,)), ((), ())), preferred_element_type=F32).astype(BF16)
    token_grad[...] = token_in[...]
    router_grad[...] = router_in[...]


def local(tokens, logits, weights, router_weight, expert_picks, cotangent):
    n = lax.axis_size("expert")
    nz = 2 ** math.ceil(math.log2(n) / 3)
    parts = PARTS
    plane = n // nz
    tok, width = tokens.shape
    piece = width // parts
    cap = expert_picks.shape[1]
    hidden = weights.shape[2]
    most = max(2 * cap // n, 16)
    share = width // n
    rs_block = (n, share) if share % 128 == 0 else (share, n)
    rs_full = (n, width) if share % 128 == 0 else (width, n)
    vmem = pl.BlockSpec(memory_space=pltpu.VMEM)
    hbm = pl.BlockSpec(memory_space=pl.ANY)
    dma = pltpu.SemaphoreType.DMA
    flops = 2 * cap * width * hidden * 2
    token_in, rows, scaled, router_in = pl.pallas_call(
        functools.partial(kernel, n, nz, most, parts),
        out_shape=(
            jax.ShapeDtypeStruct((tok, width), BF16),
            jax.ShapeDtypeStruct((parts, cap, piece), BF16),
            jax.ShapeDtypeStruct((cap, hidden), BF16),
            jax.ShapeDtypeStruct(rs_block, F32),
        ),
        in_specs=[vmem, vmem, hbm, vmem, vmem, vmem],
        out_specs=(vmem, hbm, hbm, vmem),
        scratch_shapes=[
            pltpu.VMEM((width, hidden), BF16),
            pltpu.VMEM((n, tok), F32),
            pltpu.VMEM((n, 8, 128), F32),
            pltpu.VMEM((n, 8, 128), F32),
            pltpu.VMEM((nz, plane * most, tok), BF16),
            pltpu.VMEM((nz, tok, plane * most), BF16),
            pltpu.VMEM((cap, hidden), BF16),
            pltpu.VMEM((parts, cap, piece), BF16),
            pltpu.VMEM((nz, parts, tok, piece), BF16),
            pltpu.VMEM((nz, parts, plane * most, piece), BF16),
            pltpu.VMEM((parts, n * most, piece), BF16),
            pltpu.VMEM((nz, parts, plane * most, piece), BF16),
            pltpu.VMEM((nz, parts, plane * most, piece), BF16),
            pltpu.VMEM((nz + 1, parts, tok, piece), BF16),
            pltpu.VMEM((nz, parts, tok, piece), BF16),
            pltpu.VMEM((n, 8, 128), F32),
            pltpu.VMEM((n, 8, 128), F32),
            pltpu.VMEM(rs_full, F32),
            pltpu.VMEM((n,) + rs_block, F32),
            dma, dma((2,)),
            dma((n,)), dma((n,)),
            dma((2, nz, parts)), dma((nz, parts)),
            dma((nz, parts, plane)), dma((nz, parts, plane)),
            dma((nz, parts, plane)), dma((nz, parts, plane)),
            dma((nz, parts)), dma((nz + 1, parts)),
            dma((n,)), dma((n,)),
            dma((n,)), dma((n,)),
        ],
        compiler_params=pltpu.CompilerParams(
            collective_id=0, has_side_effects=True, vmem_limit_bytes=62 * 1024 * 1024),
        cost_estimate=pl.CostEstimate(flops=flops, bytes_accessed=8 * 2 ** 20, transcendentals=0),
    )(tokens, logits.T, weights, router_weight.T, expert_picks, cotangent[0])
    block = min(256, piece)
    per = piece // block
    weight_grad, token_grad, router_grad = pl.pallas_call(
        finish,
        grid=(width // block,),
        out_shape=(
            jax.ShapeDtypeStruct((1, width, hidden), BF16),
            jax.ShapeDtypeStruct((tok, width), BF16),
            jax.ShapeDtypeStruct(rs_block, F32),
        ),
        in_specs=[
            pl.BlockSpec((1, cap, block), lambda i: (i // per, 0, i % per)),
            pl.BlockSpec((cap, hidden), lambda i: (0, 0)),
            pl.BlockSpec((tok, block), lambda i: (0, i)),
            pl.BlockSpec(rs_block, lambda i: (0, 0)),
        ],
        out_specs=(
            pl.BlockSpec((1, block, hidden), lambda i: (0, i, 0)),
            pl.BlockSpec((tok, block), lambda i: (0, i)),
            pl.BlockSpec(rs_block, lambda i: (0, 0)),
        ),
        compiler_params=pltpu.CompilerParams(vmem_limit_bytes=62 * 1024 * 1024),
        cost_estimate=pl.CostEstimate(
            flops=flops // 2, bytes_accessed=7 * 2 ** 20, transcendentals=0),
    )(rows, scaled, token_in, router_in)
    return token_grad, weight_grad, router_grad.T if share % 128 == 0 else router_grad


def solution(mesh):
    in_specs = (
        P(("dp", "expert"), None),
        P(("dp", "expert"), None),
        P("expert", None, None),
        P(),
        P(("dp", "expert"), None),
        P(("dp", "expert"), None, None),
    )
    out_specs = (
        P(("dp", "expert"), None),
        P(("dp", "expert"), None, None),
        P(("dp", "expert"), None),
    )
    return jax.shard_map(local, mesh=mesh, in_specs=in_specs, out_specs=out_specs, check_vma=False)
```
